32 devices in a mesh: groups: 2 (over x), gx: 4 (over y, core), gy: 4 (over z).
Axes of the slice: x: 2, y: 2, z: 4, core: 2. Of those that a mesh axis runs over, the one named last changes fastest.
Arguments:
- tokens: bfloat16 [64, 2, 16384], P('groups', None, 'gx'), parts along dimension 0
- norm_gain: bfloat16 [16384], P('gx'), may hold values from 0.099609375 to 1.8984375
- qkv_weight: bfloat16 [16384, 8, 18, 128], P('gx', 'gy'), may hold values from -0.046875 to 0.046875
- out_weight: bfloat16 [128, 128, 16384], P('gy', None, 'gx'), may hold values from -0.125 to 0.125
- kv_cache: bfloat16 [64, 384, 2, 8, 128], P(('groups', 'gx', 'gy')), parts along dimension 0
- lengths: int32 [64], P(('groups', 'gx', 'gy')), parts along dimension 0, may hold values from 1 to 384, as said below
- positions: int32 [64], P('groups'), parts along dimension 0, may hold values from 0 to 4095
Outputs:
- layer_out: float32 [64, 2, 16384], P(('groups', 'gy'), None, 'gx'), parts along dimension 0
The draws below stay inside these ranges and needn't reach their ends.
There are 2 independent parts, one for each index of `groups`. The reference program is written for one: setup_inputs(seed, part) draws one part's arguments, and reference() takes and returns one part's arrays. A program takes and returns all parts, laid end to end along the dimension named above; an argument that names none is the same for every part. Nothing has to cross between parts.
Inputs may be any that keep to these rules, and one draw needn't show every extreme that they name: Cache slots 0 to lengths - 1 of a row hold its earlier tokens; some row has exactly 384.
All inputs are finite; a program needn't handle non-finite values.
Results may differ from the reference program's by a relative error of at most 0.025.
Values may be sent and summed in bfloat16 or wider, within the bound.
No kernel may reach another device: no remote copies, remote signals or barrier semaphores. Data moves between devices by JAX's collectives and lax.ppermute only.
A program may use at most 192 MiB of HBM per device.

```python
import math
import jax
import jax.numpy as jnp
from jax import lax

D = 16384
HQ = 128
KV = 8
HD = 128
GQ = 16
MAXLEN = 384
ROWS = 32


def draw_tokens(key, part):
    key_base = jax.random.fold_in(key, 11)
    noise_key, scale_key = jax.random.split(key_base)
    columns = jnp.arange(D, dtype=jnp.float32) / D
    noise_part = jax.random.normal(noise_key, (ROWS, 2, D), jnp.float32)
    column_scale = jnp.exp(columns * jnp.log(10.0)) / 3.2
    row_scale = jnp.exp(jax.random.uniform(scale_key, (ROWS, 2, 1), jnp.float32, -0.7, 0.7))
    return (noise_part * column_scale * row_scale).astype(jnp.bfloat16)


def draw_kv_cache(key, part):
    key_base = jax.random.fold_in(key, 23)
    value_key = jax.random.fold_in(key_base, 0)
    entries = jax.random.normal(value_key, (ROWS, MAXLEN, 2, KV, HD), jnp.float32)
    return entries.astype(jnp.bfloat16)


def draw_lengths(key, part):
    key_base = jax.random.fold_in(key, 37)
    long_key, short_key, pick_key, top_key = jax.random.split(key_base, 4)
    long_draw = jax.random.randint(long_key, (ROWS,), 1, MAXLEN + 1)
    short_draw = jax.random.randint(short_key, (ROWS,), 1, MAXLEN // 16 + 2)
    picker = jax.random.randint(pick_key, (ROWS,), 0, 4)
    chosen = jnp.where(picker == 0, short_draw, long_draw)
    top_row = jax.random.randint(top_key, (), 0, ROWS)
    chosen = jnp.where(jnp.arange(ROWS, dtype=jnp.int32) == top_row, MAXLEN, chosen)
    return chosen.astype(jnp.int32)


def place_ends(drawn, stream_key, low, largest):
    longest = drawn.shape.index(max(drawn.shape))
    spots = []
    for shift in (0, 1):
        where = [jax.random.randint(jax.random.fold_in(stream_key, axis), (), 0, length) for axis, length in enumerate(drawn.shape)]
        where[longest] = (where[longest] + shift) % drawn.shape[longest]
        spots.append(tuple(where))
    return drawn.at[spots[0]].set(low).at[spots[1]].set(largest)


def levels(stream_key, dims, pieces, smallest, top_value):
    def one(axis_at, blocks):
        steps = jax.random.uniform(jax.random.fold_in(jax.random.fold_in(stream_key, 6), axis_at), (blocks,), jnp.float32, smallest / len(pieces), top_value / len(pieces))
        return jnp.repeat(jnp.exp(steps), dims[axis_at] // blocks).reshape((-1,) + (1,) * (len(dims) - axis_at - 1))

    level = one(*pieces[0])
    for cut in pieces[1:]:
        level = level * one(*cut)
    return level


def bell_draw(stream_key, dims, scale, most, cuts=(), kind=jnp.bfloat16):
    loudness = levels(stream_key, dims, cuts, -0.22, 0.18) if cuts else 1.0
    array = jax.random.normal(stream_key, dims, jnp.float32) * scale * loudness
    return jnp.minimum(jnp.maximum(array, -most), most).astype(kind)


def setup_inputs(seed: int = 0, part: int = 0) -> dict:
    key_of = jax.random.split(jax.random.key(seed), 8)
    part_keys = jax.random.split(jax.random.fold_in(key_of[7], part), 8)
    tokens = draw_tokens(jax.random.fold_in(jax.random.fold_in(key_of[7], part), 71), part)
    norm_gain = jnp.clip(1.0 + 0.18 * jax.random.normal(key_of[1], (D,), jnp.float32), 0.099609375, 1.8984375).astype(jnp.bfloat16)
    qkv_weight = bell_draw(key_of[2], (D, KV, GQ + 2, HD), D ** -0.5, 0.046875, ((0, 4), (1, 4)))
    out_weight = bell_draw(key_of[3], (HQ, HD, D), (GQ * HD) ** -0.5, 0.125, ((0, 4), (2, 4)))
    kv_cache = draw_kv_cache(jax.random.fold_in(jax.random.fold_in(key_of[7], part), 71), part)
    lengths = draw_lengths(jax.random.fold_in(jax.random.fold_in(key_of[7], part), 71), part)
    positions = place_ends(jax.random.randint(part_keys[6], (ROWS,), 0, 4096), jax.random.fold_in(part_keys[6], 1), 0, 4095).astype(jnp.int32)
    return dict(tokens=tokens, norm_gain=norm_gain, qkv_weight=qkv_weight, out_weight=out_weight, kv_cache=kv_cache, lengths=lengths, positions=positions)


norm_eps = 1e-05
rope_base = 500000.0

def rotate(values, places):
    half_dim = values.shape[-1] // 2
    index_half = jnp.arange(half_dim, dtype=jnp.float32)
    frequency = rope_base ** (-2.0 * index_half / values.shape[-1])
    angles = places[..., None] * frequency
    cosine = jnp.cos(angles)
    sine_part = jnp.sin(angles)
    front_half = values[..., :half_dim]
    back_half = values[..., half_dim:]
    return jnp.concatenate([front_half * cosine - back_half * sine_part, back_half * cosine + front_half * sine_part], axis=-1)

def attend(queries, key_new, value_new, cache_rows, length):
    scale_factor = 1.0 / math.sqrt(queries.shape[-1])
    query_wide = queries.astype(jnp.float32)
    old_keys = cache_rows[:, :, 0].astype(jnp.float32)
    old_values = cache_rows[:, :, 1].astype(jnp.float32)
    scores_old = jnp.einsum('rtgid,rsgd->rtgis', query_wide, old_keys) * scale_factor
    slot_ids = jnp.arange(cache_rows.shape[1], dtype=jnp.int32)
    visible = slot_ids[None, :] < length[:, None]
    scores_old = jnp.where(visible[:, None, None, None, :], scores_old, -1e+30)
    scores_new = jnp.einsum('rtgid,rugd->rtgiu', query_wide, key_new.astype(jnp.float32)) * scale_factor
    token_ids = jnp.arange(queries.shape[1], dtype=jnp.int32)
    causal = token_ids[:, None] >= token_ids[None, :]
    scores_new = jnp.where(causal[None, :, None, None, :], scores_new, -1e+30)
    highest = jnp.maximum(lax.optimization_barrier(jnp.max(scores_old, axis=-1)), lax.optimization_barrier(jnp.max(scores_new, axis=-1)))
    expo_old = jnp.exp(scores_old - highest[..., None])
    expo_new = jnp.exp(scores_new - highest[..., None])
    denominator = lax.optimization_barrier(jnp.sum(expo_old, axis=-1)) + lax.optimization_barrier(jnp.sum(expo_new, axis=-1))
    weight_old = (expo_old / denominator[..., None]).astype(jnp.bfloat16)
    weight_new = (expo_new / denominator[..., None]).astype(jnp.bfloat16)
    attended = jnp.einsum('rtgis,rsgd->rtgid', weight_old.astype(jnp.float32), old_values)
    attended = attended + jnp.einsum('rtgiu,rugd->rtgid', weight_new.astype(jnp.float32), value_new.astype(jnp.float32))
    return attended.astype(jnp.bfloat16)

def reference(tokens, norm_gain, qkv_weight, out_weight, kv_cache, lengths, positions):
    tokens_wide = tokens.astype(jnp.float32)
    hidden = (tokens_wide * norm_gain.astype(jnp.float32)).astype(jnp.bfloat16)
    inv_rms = lax.rsqrt(lax.optimization_barrier(jnp.sum(tokens_wide * tokens_wide, axis=-1)) / D + norm_eps)
    projected = jnp.dot(hidden.reshape(ROWS * 2, D), qkv_weight.reshape(D, KV * (GQ + 2) * HD), preferred_element_type=jnp.float32)
    projected = projected.reshape(ROWS, 2, KV, GQ + 2, HD) * inv_rms[:, :, None, None, None]
    places = (positions[:, None] + jnp.arange(2, dtype=jnp.int32)[None, :]).astype(jnp.float32)
    queries = rotate(projected[:, :, :, :GQ], places[:, :, None, None]).astype(jnp.bfloat16)
    key_new = rotate(projected[:, :, :, GQ], places[:, :, None]).astype(jnp.bfloat16)
    value_new = projected[:, :, :, GQ + 1].astype(jnp.bfloat16)

    def one_row(packed):
        return attend(packed[0], packed[1], packed[2], packed[3], packed[4])
    attended = lax.map(one_row, (queries[:, None], key_new[:, None], value_new[:, None], kv_cache[:, None], lengths[:, None]))
    attended = attended.reshape(ROWS * 2, HQ * HD)
    update = jnp.dot(attended, out_weight.reshape(HQ * HD, D), preferred_element_type=jnp.float32)
    return tokens_wide + update.reshape(ROWS, 2, D)
```

```python
import functools
import math

import jax
import jax.numpy as jnp
from jax import lax
from jax.experimental import pallas as pl
from jax.experimental.pallas import tpu as pltpu
from jax.sharding import PartitionSpec as P

D = 16384


norm_eps = 1e-05
rope_base = 500000.0


def rotate(values, places):
    half_dim = values.shape[-1] // 2
    index_half = jnp.arange(half_dim, dtype=jnp.float32)
    frequency = rope_base ** (-2.0 * index_half / values.shape[-1])
    angles = places[..., None] * frequency
    cosine = jnp.cos(angles)
    sine_part = jnp.sin(angles)
    front_half = values[..., :half_dim]
    back_half = values[..., half_dim:]
    return jnp.concatenate(
        [front_half * cosine - back_half * sine_part, back_half * cosine + front_half * sine_part],
        axis=-1,
    )


def finish(projected, positions, first_row, row_count):
    group_size = projected.shape[3] - 2
    placed = lax.dynamic_slice_in_dim(positions, first_row, row_count, 0)
    places = (placed[:, None] + jnp.arange(2, dtype=jnp.int32)[None, :]).astype(jnp.float32)
    queries = rotate(projected[:, :, :, :group_size], places[:, :, None, None])
    key_new = rotate(projected[:, :, :, group_size : group_size + 1], places[:, :, None, None])
    value_new = projected[:, :, :, group_size + 1 :]
    return jnp.concatenate([queries, key_new, value_new], axis=3).astype(jnp.bfloat16)


def attend(queries, key_new, value_new, cache_rows, length):
    scale_factor = 1.0 / math.sqrt(queries.shape[-1])
    scores_old = (
        jnp.einsum(
            "rtgid,rsgd->rtgis", queries, cache_rows[:, :, 0], preferred_element_type=jnp.float32
        )
        * scale_factor
    )
    slot_ids = jnp.arange(cache_rows.shape[1], dtype=jnp.int32)
    visible = slot_ids[None, :] < length[:, None]
    scores_old = jnp.where(visible[:, None, None, None, :], scores_old, -1e30)
    scores_new = (
        jnp.einsum("rtgid,rugd->rtgiu", queries, key_new, preferred_element_type=jnp.float32)
        * scale_factor
    )
    token_ids = jnp.arange(queries.shape[1], dtype=jnp.int32)
    causal = token_ids[:, None] >= token_ids[None, :]
    scores_new = jnp.where(causal[None, :, None, None, :], scores_new, -1e30)
    highest = jnp.maximum(jnp.max(scores_old, axis=-1), jnp.max(scores_new, axis=-1))
    expo_old = jnp.exp(scores_old - highest[..., None])
    expo_new = jnp.exp(scores_new - highest[..., None])
    denominator = jnp.sum(expo_old, axis=-1) + jnp.sum(expo_new, axis=-1)
    weight_old = (expo_old / denominator[..., None]).astype(jnp.bfloat16)
    weight_new = (expo_new / denominator[..., None]).astype(jnp.bfloat16)
    attended = jnp.einsum(
        "rtgis,rsgd->rtgid", weight_old, cache_rows[:, :, 1], preferred_element_type=jnp.float32
    )
    attended = attended + jnp.einsum(
        "rtgiu,rugd->rtgid", weight_new, value_new, preferred_element_type=jnp.float32
    )
    return attended.astype(jnp.bfloat16)


def shift_pairs(count, shift):
    return [(i, (i + shift) % count) for i in range(count)]


def pick_block(features):
    block = features
    while block > 1024 and block % 2 == 0:
        block //= 2
    return block


def project_kernel(axis_size, index_ref, tokens_ref, gain_ref, weight_ref, *rest):
    outs, (spread_ref, total_ref, square_ref) = rest[:axis_size], rest[axis_size:]
    step = pl.program_id(0)
    token_count, block = tokens_ref.shape
    heads, groups, head_dim = weight_ref.shape[1:]
    tokens_wide = tokens_ref[...].astype(jnp.float32)
    hidden = (tokens_wide * gain_ref[...].astype(jnp.float32)).astype(jnp.bfloat16)
    lanes = 128
    wide = lanes * groups
    place = lax.broadcasted_iota(jnp.int32, (lanes, wide * groups), 0)
    column = lax.broadcasted_iota(jnp.int32, (lanes, wide * groups), 1)
    group_of = column // wide
    spread = (column - group_of * wide == place * groups + group_of).astype(jnp.bfloat16)
    squares = jnp.zeros((token_count, lanes), jnp.float32)
    for i in range(block // lanes):
        piece = tokens_wide[:, i * lanes : (i + 1) * lanes]
        squares = squares + piece * piece
        out = jnp.dot(
            hidden[:, i * lanes : (i + 1) * lanes], spread, preferred_element_type=jnp.float32
        ).astype(jnp.bfloat16)
        for g in range(groups):
            spread_ref[g * token_count : (g + 1) * token_count, i * wide : (i + 1) * wide] = out[
                :, g * wide : (g + 1) * wide
            ]

    @pl.when(step == 0)
    def _():
        square_ref[...] = squares

    @pl.when(step > 0)
    def _():
        square_ref[...] += squares

    for pair in range(heads // 2):
        weights = jnp.concatenate(
            [weight_ref[:, 2 * pair + i].reshape(block * groups, head_dim) for i in range(2)],
            axis=1,
        )
        term = jnp.dot(spread_ref[...], weights, preferred_element_type=jnp.float32)

        @pl.when(step == 0)
        def _():
            total_ref[pair] = term

        @pl.when(step > 0)
        def _():
            total_ref[pair] += term

    @pl.when(step == pl.num_programs(0) - 1)
    def _():
        rows = token_count // axis_size
        lane = lax.broadcasted_iota(jnp.int32, (rows, lanes), 1)
        for shift in range(axis_size):
            first = lax.rem(index_ref[0] + shift, axis_size) * rows
            first = pl.multiple_of(first, rows)
            own = outs[shift]
            for g in range(groups):
                for pair in range(heads // 2):
                    own[g, :, pair * 2 * head_dim : (pair + 1) * 2 * head_dim] = total_ref[
                        pair, pl.ds(g * token_count + first, rows), :
                    ].astype(own.dtype)
                total = jnp.sum(square_ref[pl.ds(first, rows), :], axis=1, keepdims=True)
                high = total.astype(jnp.bfloat16).astype(jnp.float32)
                middle = (total - high).astype(jnp.bfloat16).astype(jnp.float32)
                low = total - high - middle
                own[g, :, heads * head_dim :] = jnp.where(
                    lane == 0, high, jnp.where(lane == 1, middle, jnp.where(lane == 2, low, 0.0))
                ).astype(own.dtype)


def project(tokens, norm_gain, qkv_weight, axis_size, index):
    token_count, features = tokens.shape
    _, groups, heads, head_dim = qkv_weight.shape
    block = pick_block(features)
    rows = token_count // axis_size
    width = heads * head_dim + 128
    return pl.pallas_call(
        functools.partial(project_kernel, axis_size),
        grid_spec=pltpu.PrefetchScalarGridSpec(
            num_scalar_prefetch=1,
            grid=(features // block,),
            in_specs=[
                pl.BlockSpec((token_count, block), lambda k, _: (0, k)),
                pl.BlockSpec((1, block), lambda k, _: (0, k)),
                pl.BlockSpec((block, heads, groups, head_dim), lambda k, _: (k, 0, 0, 0)),
            ],
            out_specs=[pl.BlockSpec((groups, rows, width), lambda k, _: (0, 0, 0))] * axis_size,
            scratch_shapes=[
                pltpu.VMEM((groups * token_count, block * groups), jnp.bfloat16),
                pltpu.VMEM((heads // 2, groups * token_count, 2 * head_dim), jnp.float32),
                pltpu.VMEM((token_count, 128), jnp.float32),
            ],
        ),
        out_shape=[
            jax.ShapeDtypeStruct((groups, rows, width), jnp.bfloat16 if s else jnp.float32)
            for s in range(axis_size)
        ],
        compiler_params=pltpu.CompilerParams(vmem_limit_bytes=48 * 2**20),
        cost_estimate=pl.CostEstimate(
            flops=2 * qkv_weight.size * token_count,
            bytes_accessed=qkv_weight.size * 2,
            transcendentals=0,
        ),
        name="project",
    )(index[None], tokens, norm_gain[None, :], jnp.transpose(qkv_weight, (0, 2, 1, 3)))


def outward_kernel(axis_size, index_ref, attended_ref, weight_ref, *rest):
    outs, total_ref = rest[:axis_size], rest[axis_size]
    token_count, depth = attended_ref.shape
    rows = token_count // axis_size
    block = pick_block(depth)
    for k in range(depth // block):
        term = jnp.dot(
            attended_ref[:, k * block : (k + 1) * block],
            weight_ref[k * block : (k + 1) * block, :],
            preferred_element_type=jnp.float32,
        )
        if k == 0:
            total_ref[...] = term
        else:
            total_ref[...] += term
    for shift in range(axis_size):
        first = pl.multiple_of(lax.rem(index_ref[0] + shift, axis_size) * rows, rows)
        outs[shift][...] = total_ref[pl.ds(first, rows), :].astype(outs[shift].dtype)


def outward(attended, out_flat, axis_size, index):
    token_count, depth = attended.shape
    width = out_flat.shape[1]
    block = pick_block(width)
    rows = token_count // axis_size
    return pl.pallas_call(
        functools.partial(outward_kernel, axis_size),
        grid_spec=pltpu.PrefetchScalarGridSpec(
            num_scalar_prefetch=1,
            grid=(width // block,),
            in_specs=[
                pl.BlockSpec((token_count, depth), lambda j, _: (0, 0)),
                pl.BlockSpec((depth, block), lambda j, _: (0, j)),
            ],
            out_specs=[pl.BlockSpec((rows, block), lambda j, _: (0, j))] * axis_size,
            scratch_shapes=[pltpu.VMEM((token_count, block), jnp.float32)],
        ),
        out_shape=[
            jax.ShapeDtypeStruct((rows, width), jnp.bfloat16 if s else jnp.float32)
            for s in range(axis_size)
        ],
        compiler_params=pltpu.CompilerParams(vmem_limit_bytes=48 * 2**20),
        cost_estimate=pl.CostEstimate(
            flops=2 * out_flat.size * token_count,
            bytes_accessed=out_flat.size * 2,
            transcendentals=0,
        ),
        name="outward",
    )(index[None], attended, out_flat)


def sum_pieces(pieces, axis):
    count = len(pieces)
    total = pieces[0]
    landed = [lax.ppermute(pieces[s], axis, shift_pairs(count, s)) for s in range(1, count)]
    for piece in landed:
        total = total + piece.astype(jnp.float32)
    return total


def body(tokens, norm_gain, qkv_weight, out_weight, kv_cache, lengths, positions):
    rows_local = kv_cache.shape[0]
    width_devices = lax.axis_size("gx")
    head_devices = lax.axis_size("gy")
    width_index = lax.axis_index("gx")
    head_index = lax.axis_index("gy")
    total_rows = tokens.shape[0]
    local_width = tokens.shape[2]
    groups_local, group_width, head_dim = qkv_weight.shape[1:]
    group_size = group_width - 2
    block_rows = rows_local * head_devices
    pieces = project(
        tokens.reshape(total_rows * 2, local_width),
        norm_gain,
        qkv_weight,
        width_devices,
        width_index,
    )
    block_sum = sum_pieces(pieces, "gx")
    flat = group_width * head_dim
    block_squares = jnp.sum(block_sum[0, :, flat : flat + 3], axis=-1)
    inv_rms = lax.rsqrt(block_squares / D + norm_eps)
    projected = (block_sum[:, :, :flat] * inv_rms[None, :, None]).reshape(
        groups_local, block_rows, 2, group_width, head_dim
    )
    projected = jnp.transpose(projected, (1, 2, 0, 3, 4))
    ready = finish(projected, positions, width_index * block_rows, block_rows)
    packed = lax.all_to_all(ready, "gy", split_axis=0, concat_axis=2, tiled=True)
    queries = packed[:, :, :, :group_size]
    key_new = packed[:, :, :, group_size]
    value_new = packed[:, :, :, group_size + 1]
    attended = attend(queries, key_new, value_new, kv_cache, lengths)
    regrouped = lax.all_to_all(attended, "gy", split_axis=2, concat_axis=0, tiled=True)
    out_flat = out_weight.reshape(-1, local_width)
    row_piece = lax.all_gather(regrouped, "gx", axis=0, tiled=True)
    piece_rows = row_piece.shape[0]
    parts = outward(row_piece.reshape(piece_rows * 2, -1), out_flat, head_devices, head_index)
    row_share = total_rows // head_devices
    own_sum = sum_pieces(parts, "gy").reshape(row_share, 2, local_width)
    residual = lax.dynamic_slice_in_dim(tokens, head_index * row_share, row_share, 0).astype(
        jnp.float32
    )
    return residual + own_sum


def solution(mesh):
    return jax.shard_map(
        body,
        mesh=mesh,
        in_specs=(
            P("groups", None, "gx"),
            P("gx"),
            P("gx", "gy", None, None),
            P("gy", None, "gx"),
            P(("groups", "gx", "gy"), None, None, None, None),
            P(("groups", "gx", "gy")),
            P("groups"),
        ),
        out_specs=P(("groups", "gy"), None, "gx"),
        check_vma=False,
    )
```

```python
import functools
import math

import jax
import jax.numpy as jnp
from jax import lax
from jax.experimental import pallas as pl
from jax.experimental.pallas import tpu as pltpu
from jax.sharding import PartitionSpec as P

D = 16384


norm_eps = 1e-05
rope_base = 500000.0
PROJECT_BLOCK = 512
PROJECT_SLOTS = 3


def rotate(values, places):
    half_dim = values.shape[-1] // 2
    index_half = jnp.arange(half_dim, dtype=jnp.float32)
    frequency = rope_base ** (-2.0 * index_half / values.shape[-1])
    angles = places[..., None] * frequency
    cosine = jnp.cos(angles)
    sine_part = jnp.sin(angles)
    front_half = values[..., :half_dim]
    back_half = values[..., half_dim:]
    return jnp.concatenate(
        [front_half * cosine - back_half * sine_part, back_half * cosine + front_half * sine_part],
        axis=-1,
    )


def finish(projected, positions, first_row, row_count):
    group_size = projected.shape[3] - 2
    placed = lax.dynamic_slice_in_dim(positions, first_row, row_count, 0)
    places = (placed[:, None] + jnp.arange(2, dtype=jnp.int32)[None, :]).astype(jnp.float32)
    queries = rotate(projected[:, :, :, :group_size], places[:, :, None, None])
    key_new = rotate(projected[:, :, :, group_size : group_size + 1], places[:, :, None, None])
    value_new = projected[:, :, :, group_size + 1 :]
    return jnp.concatenate([queries, key_new, value_new], axis=3).astype(jnp.bfloat16)


def attend(queries, key_new, value_new, cache_rows, length):
    scale_factor = 1.0 / math.sqrt(queries.shape[-1])
    scores_old = (
        jnp.einsum(
            "rtgid,rsgd->rtgis", queries, cache_rows[:, :, 0], preferred_element_type=jnp.float32
        )
        * scale_factor
    )
    slot_ids = jnp.arange(cache_rows.shape[1], dtype=jnp.int32)
    visible = slot_ids[None, :] < length[:, None]
    scores_old = jnp.where(visible[:, None, None, None, :], scores_old, -1e30)
    scores_new = (
        jnp.einsum("rtgid,rugd->rtgiu", queries, key_new, preferred_element_type=jnp.float32)
        * scale_factor
    )
    token_ids = jnp.arange(queries.shape[1], dtype=jnp.int32)
    causal = token_ids[:, None] >= token_ids[None, :]
    scores_new = jnp.where(causal[None, :, None, None, :], scores_new, -1e30)
    highest = jnp.maximum(jnp.max(scores_old, axis=-1), jnp.max(scores_new, axis=-1))
    expo_old = jnp.exp(scores_old - highest[..., None])
    expo_new = jnp.exp(scores_new - highest[..., None])
    denominator = jnp.sum(expo_old, axis=-1) + jnp.sum(expo_new, axis=-1)
    weight_old = (expo_old / denominator[..., None]).astype(jnp.bfloat16)
    weight_new = (expo_new / denominator[..., None]).astype(jnp.bfloat16)
    attended = jnp.einsum(
        "rtgis,rsgd->rtgid", weight_old, cache_rows[:, :, 1], preferred_element_type=jnp.float32
    )
    attended = attended + jnp.einsum(
        "rtgiu,rugd->rtgid", weight_new, value_new, preferred_element_type=jnp.float32
    )
    return attended.astype(jnp.bfloat16)


def shift_pairs(count, shift):
    return [(i, (i + shift) % count) for i in range(count)]


def pick_block(features):
    block = features
    while block > 1024 and block % 2 == 0:
        block //= 2
    return block


def split_squares(total, lanes):
    high = total.astype(jnp.bfloat16).astype(jnp.float32)
    middle = (total - high).astype(jnp.bfloat16).astype(jnp.float32)
    low = total - high - middle
    lane = lax.broadcasted_iota(jnp.int32, (total.shape[0], lanes), 1)
    return jnp.where(
        lane == 0, high, jnp.where(lane == 1, middle, jnp.where(lane == 2, low, 0.0))
    )


def project_kernel(axis_size, block, slots, index_ref, tokens_ref, gain_ref, weight_ref, *rest):
    outs, rest = rest[:axis_size], rest[axis_size:]
    hidden_ref, spread_ref, total_ref, sum_ref, gain_wide, buffer, arrived = rest
    total_rows, pair_rows, features = tokens_ref.shape
    token_count = total_rows * pair_rows
    pairs, mix, head_dim = weight_ref.shape[1:]
    groups = mix // 2
    steps = features // block
    lanes = 128

    def fetch(step, slot):
        return pltpu.make_async_copy(
            weight_ref.at[pl.ds(step * block, block)], buffer.at[slot], arrived.at[slot]
        )

    for step in range(min(slots, steps)):
        fetch(step, step).start()

    wide = lanes * mix
    place = lax.broadcasted_iota(jnp.int32, (lanes, wide), 0)
    column = lax.broadcasted_iota(jnp.int32, (lanes, wide), 1)
    repeat = (column // mix == place).astype(jnp.bfloat16)
    member_of = lax.rem(lax.broadcasted_iota(jnp.int32, (token_count, wide), 1), mix)
    members = [(member_of == m).astype(jnp.bfloat16) for m in range(mix)]
    gain_wide[...] = gain_ref[...].astype(jnp.float32)
    squares = jnp.zeros((token_count, lanes), jnp.float32)
    group = 4
    for i in range(0, features // lanes, group):
        for j in range(group):
            at = (i + j) * lanes
            piece = tokens_ref[:, :, at : at + lanes].reshape(token_count, lanes)
            piece = piece.astype(jnp.float32)
            squares = squares + piece * piece
            hidden_ref[j * token_count : (j + 1) * token_count, :] = (
                piece * gain_wide[i + j : i + j + 1, :]
            ).astype(jnp.bfloat16)
        repeated = jnp.dot(hidden_ref[...], repeat, preferred_element_type=jnp.float32)
        repeated = repeated.astype(jnp.bfloat16)
        for j in range(group):
            for m in range(mix):
                spread_ref[
                    m * token_count : (m + 1) * token_count, (i + j) * wide : (i + j + 1) * wide
                ] = repeated[j * token_count : (j + 1) * token_count, :] * members[m]
    total_ref[...] = jnp.zeros_like(total_ref)

    @pl.loop(0, steps)
    def _(step):
        slot = lax.rem(step, slots)
        fetch(step, slot).wait()
        left = spread_ref.at[:, pl.ds(pl.multiple_of(step * block * mix, 128), block * mix)]
        for first in range(0, pairs, 4):
            count = min(4, pairs - first)
            weights = [
                buffer[slot, :, first + i].reshape(block * mix, head_dim) for i in range(count)
            ]
            weights = jnp.concatenate(weights, axis=1) if count > 1 else weights[0]
            total_ref[:, first * head_dim : (first + count) * head_dim] += jnp.dot(
                left[...], weights, preferred_element_type=jnp.float32
            )

        @pl.when(step + slots < steps)
        def _():
            fetch(step + slots, slot).start()

    rows = token_count // axis_size
    sum_ref[...] = split_squares(jnp.sum(squares, axis=1, keepdims=True), lanes)
    for shift in range(axis_size):
        owner = lax.rem(index_ref[0] + shift, axis_size)
        first = pl.multiple_of(owner * rows, rows)
        own = outs[shift]
        for g in range(groups):
            for head in range(2 * pairs):
                start = ((head % 2) * groups + g) * token_count
                lane = (head // 2) * head_dim
                own[g, :, head * head_dim : (head + 1) * head_dim] = total_ref[
                    pl.ds(start + first, rows), lane : lane + head_dim
                ].astype(own.dtype)
            own[g, :, 2 * pairs * head_dim :] = sum_ref[pl.ds(first, rows), :].astype(own.dtype)


def project(tokens, norm_gain, qkv_weight, axis_size, index):
    features, groups, heads, head_dim = qkv_weight.shape
    token_count = tokens.shape[0] * tokens.shape[1]
    mix = 2 * groups
    pairs = heads // 2
    block = min(features, PROJECT_BLOCK)
    slots = PROJECT_SLOTS
    rows = token_count // axis_size
    width = heads * head_dim + 128
    weight = jnp.transpose(qkv_weight, (0, 2, 1, 3)).reshape(features, pairs, mix, head_dim)
    return pl.pallas_call(
        functools.partial(project_kernel, axis_size, block, slots),
        in_specs=[
            pl.BlockSpec(memory_space=pltpu.SMEM),
            pl.BlockSpec(memory_space=pltpu.VMEM),
            pl.BlockSpec(memory_space=pltpu.VMEM),
            pl.BlockSpec(memory_space=pl.ANY),
        ],
        out_specs=[pl.BlockSpec(memory_space=pltpu.VMEM)] * axis_size,
        scratch_shapes=[
            pltpu.VMEM((4 * token_count, 128), jnp.bfloat16),
            pltpu.VMEM((mix * token_count, features * mix), jnp.bfloat16),
            pltpu.VMEM((mix * token_count, pairs * head_dim), jnp.float32),
            pltpu.VMEM((token_count, 128), jnp.float32),
            pltpu.VMEM((features // 128, 128), jnp.float32),
            pltpu.VMEM((slots, block, pairs, mix, head_dim), jnp.bfloat16),
            pltpu.SemaphoreType.DMA((slots,)),
        ],
        out_shape=[
            jax.ShapeDtypeStruct((groups, rows, width), jnp.bfloat16 if s else jnp.float32)
            for s in range(axis_size)
        ],
        compiler_params=pltpu.CompilerParams(vmem_limit_bytes=48 * 2**20),
        cost_estimate=pl.CostEstimate(
            flops=2 * qkv_weight.size * token_count,
            bytes_accessed=qkv_weight.size * 2,
            transcendentals=0,
        ),
        name="project",
    )(index[None], tokens, norm_gain.reshape(-1, 128), weight)


def outward_kernel(axis_size, index_ref, attended_ref, weight_ref, *rest):
    outs, total_ref = rest[:axis_size], rest[axis_size]
    token_count, depth = attended_ref.shape
    rows = token_count // axis_size
    block = pick_block(depth)
    for k in range(depth // block):
        term = jnp.dot(
            attended_ref[:, k * block : (k + 1) * block],
            weight_ref[k * block : (k + 1) * block, :],
            preferred_element_type=jnp.float32,
        )
        if k == 0:
            total_ref[...] = term
        else:
            total_ref[...] += term
    for shift in range(axis_size):
        first = pl.multiple_of(lax.rem(index_ref[0] + shift, axis_size) * rows, rows)
        outs[shift][...] = total_ref[pl.ds(first, rows), :].astype(outs[shift].dtype)


def outward(attended, out_flat, axis_size, index):
    token_count, depth = attended.shape
    width = out_flat.shape[1]
    block = pick_block(width)
    rows = token_count // axis_size
    return pl.pallas_call(
        functools.partial(outward_kernel, axis_size),
        grid_spec=pltpu.PrefetchScalarGridSpec(
            num_scalar_prefetch=1,
            grid=(width // block,),
            in_specs=[
                pl.BlockSpec((token_count, depth), lambda j, _: (0, 0)),
                pl.BlockSpec((depth, block), lambda j, _: (0, j)),
            ],
            out_specs=[pl.BlockSpec((rows, block), lambda j, _: (0, j))] * axis_size,
            scratch_shapes=[pltpu.VMEM((token_count, block), jnp.float32)],
        ),
        out_shape=[
            jax.ShapeDtypeStruct((rows, width), jnp.bfloat16 if s else jnp.float32)
            for s in range(axis_size)
        ],
        compiler_params=pltpu.CompilerParams(vmem_limit_bytes=48 * 2**20),
        cost_estimate=pl.CostEstimate(
            flops=2 * out_flat.size * token_count,
            bytes_accessed=out_flat.size * 2,
            transcendentals=0,
        ),
        name="outward",
    )(index[None], attended, out_flat)


def sum_pieces(pieces, axis):
    count = len(pieces)
    total = pieces[0]
    landed = [lax.ppermute(pieces[s], axis, shift_pairs(count, s)) for s in range(1, count)]
    for piece in landed:
        total = total + piece.astype(jnp.float32)
    return total


def body(tokens, norm_gain, qkv_weight, out_weight, kv_cache, lengths, positions):
    rows_local = kv_cache.shape[0]
    width_devices = lax.axis_size("gx")
    head_devices = lax.axis_size("gy")
    width_index = lax.axis_index("gx")
    head_index = lax.axis_index("gy")
    total_rows = tokens.shape[0]
    local_width = tokens.shape[2]
    groups_local, group_width, head_dim = qkv_weight.shape[1:]
    group_size = group_width - 2
    block_rows = rows_local * head_devices
    pieces = project(
        tokens,
        norm_gain,
        qkv_weight,
        width_devices,
        width_index,
    )
    block_sum = sum_pieces(pieces, "gx")
    flat = group_width * head_dim
    block_squares = jnp.sum(block_sum[0, :, flat : flat + 3], axis=-1)
    inv_rms = lax.rsqrt(block_squares / D + norm_eps)
    projected = (block_sum[:, :, :flat] * inv_rms[None, :, None]).reshape(
        groups_local, block_rows, 2, group_width, head_dim
    )
    projected = jnp.transpose(projected, (1, 2, 0, 3, 4))
    ready = finish(projected, positions, width_index * block_rows, block_rows)
    packed = lax.all_to_all(ready, "gy", split_axis=0, concat_axis=2, tiled=True)
    queries = packed[:, :, :, :group_size]
    key_new = packed[:, :, :, group_size]
    value_new = packed[:, :, :, group_size + 1]
    attended = attend(queries, key_new, value_new, kv_cache, lengths)
    regrouped = lax.all_to_all(attended, "gy", split_axis=2, concat_axis=0, tiled=True)
    out_flat = out_weight.reshape(-1, local_width)
    row_piece = lax.all_gather(regrouped, "gx", axis=0, tiled=True)
    piece_rows = row_piece.shape[0]
    parts = outward(row_piece.reshape(piece_rows * 2, -1), out_flat, head_devices, head_index)
    row_share = total_rows // head_devices
    own_sum = sum_pieces(parts, "gy").reshape(row_share, 2, local_width)
    residual = lax.dynamic_slice_in_dim(tokens, head_index * row_share, row_share, 0).astype(
        jnp.float32
    )
    return residual + own_sum


def solution(mesh):
    return jax.shard_map(
        body,
        mesh=mesh,
        in_specs=(
            P("groups", None, "gx"),
            P("gx"),
            P("gx", "gy", None, None),
            P("gy", None, "gx"),
            P(("groups", "gx", "gy"), None, None, None, None),
            P(("groups", "gx", "gy")),
            P("groups"),
        ),
        out_specs=P(("groups", "gy"), None, "gx"),
        check_vma=False,
    )
```

```python
import functools
import math

import jax
import jax.numpy as jnp
from jax import lax
from jax.experimental import pallas as pl
from jax.experimental.pallas import tpu as pltpu
from jax.sharding import PartitionSpec as P

D = 16384


norm_eps = 1e-05
rope_base = 500000.0
PROJECT_BLOCK = 512
PROJECT_SLOTS = 3
SMALL_LIMIT = 12 * 2**20


def shift_pairs(count, shift):
    return [(i, (i + shift) % count) for i in range(count)]


def pick_block(features):
    block = features
    while block > 1024 and block % 2 == 0:
        block //= 2
    return block


def split_squares(total, lanes):
    high = total.astype(jnp.bfloat16).astype(jnp.float32)
    middle = (total - high).astype(jnp.bfloat16).astype(jnp.float32)
    low = total - high - middle
    lane = lax.broadcasted_iota(jnp.int32, (total.shape[0], lanes), 1)
    return jnp.where(
        lane == 0, high, jnp.where(lane == 1, middle, jnp.where(lane == 2, low, 0.0))
    )


def project_kernel(axis_size, block, slots, index_ref, tokens_ref, gain_ref, weight_ref, *rest):
    outs, rest = rest[:axis_size], rest[axis_size:]
    hidden_ref, spread_ref, total_ref, sum_ref, gain_wide, buffer, arrived = rest
    total_rows, pair_rows, features = tokens_ref.shape
    token_count = total_rows * pair_rows
    pairs, mix, head_dim = weight_ref.shape[1:]
    groups = mix // 2
    steps = features // block
    lanes = 128

    def fetch(step, slot):
        return pltpu.make_async_copy(
            weight_ref.at[pl.ds(step * block, block)], buffer.at[slot], arrived.at[slot]
        )

    for step in range(min(slots, steps)):
        fetch(step, step).start()

    wide = lanes * mix
    place = lax.broadcasted_iota(jnp.int32, (lanes, wide), 0)
    column = lax.broadcasted_iota(jnp.int32, (lanes, wide), 1)
    repeat = (column // mix == place).astype(jnp.bfloat16)
    member_of = lax.rem(lax.broadcasted_iota(jnp.int32, (token_count, wide), 1), mix)
    members = [(member_of == m).astype(jnp.bfloat16) for m in range(mix)]
    gain_wide[...] = gain_ref[...].astype(jnp.float32)
    squares = jnp.zeros((token_count, lanes), jnp.float32)
    group = 4
    for i in range(0, features // lanes, group):
        for j in range(group):
            at = (i + j) * lanes
            piece = tokens_ref[:, :, at : at + lanes].reshape(token_count, lanes)
            piece = piece.astype(jnp.float32)
            squares = squares + piece * piece
            hidden_ref[j * token_count : (j + 1) * token_count, :] = (
                piece * gain_wide[i + j : i + j + 1, :]
            ).astype(jnp.bfloat16)
        repeated = jnp.dot(hidden_ref[...], repeat, preferred_element_type=jnp.float32)
        repeated = repeated.astype(jnp.bfloat16)
        for j in range(group):
            for m in range(mix):
                spread_ref[
                    m * token_count : (m + 1) * token_count, (i + j) * wide : (i + j + 1) * wide
                ] = repeated[j * token_count : (j + 1) * token_count, :] * members[m]
    total_ref[...] = jnp.zeros_like(total_ref)

    @pl.loop(0, steps)
    def _(step):
        slot = lax.rem(step, slots)
        fetch(step, slot).wait()
        left = spread_ref.at[:, pl.ds(pl.multiple_of(step * block * mix, 128), block * mix)]
        for first in range(0, pairs, 4):
            count = min(4, pairs - first)
            weights = [
                buffer[slot, :, first + i].reshape(block * mix, head_dim) for i in range(count)
            ]
            weights = jnp.concatenate(weights, axis=1) if count > 1 else weights[0]
            total_ref[:, first * head_dim : (first + count) * head_dim] += jnp.dot(
                left[...], weights, preferred_element_type=jnp.float32
            )

        @pl.when(step + slots < steps)
        def _():
            fetch(step + slots, slot).start()

    rows = token_count // axis_size
    sum_ref[...] = split_squares(jnp.sum(squares, axis=1, keepdims=True), lanes)
    for shift in range(axis_size):
        owner = lax.rem(index_ref[0] + shift, axis_size)
        first = pl.multiple_of(owner * rows, rows)
        own = outs[shift]
        for g in range(groups):
            for head in range(2 * pairs):
                start = ((head % 2) * groups + g) * token_count
                lane = (head // 2) * head_dim
                own[g, :, head * head_dim : (head + 1) * head_dim] = total_ref[
                    pl.ds(start + first, rows), lane : lane + head_dim
                ].astype(own.dtype)
            own[g, :, 2 * pairs * head_dim :] = sum_ref[pl.ds(first, rows), :].astype(own.dtype)


def project(tokens, norm_gain, qkv_weight, axis_size, index):
    features, groups, heads, head_dim = qkv_weight.shape
    token_count = tokens.shape[0] * tokens.shape[1]
    mix = 2 * groups
    pairs = heads // 2
    block = min(features, PROJECT_BLOCK)
    slots = PROJECT_SLOTS
    rows = token_count // axis_size
    width = heads * head_dim + 128
    weight = jnp.transpose(qkv_weight, (0, 2, 1, 3)).reshape(features, pairs, mix, head_dim)
    return pl.pallas_call(
        functools.partial(project_kernel, axis_size, block, slots),
        in_specs=[
            pl.BlockSpec(memory_space=pltpu.SMEM),
            pl.BlockSpec(memory_space=pltpu.VMEM),
            pl.BlockSpec(memory_space=pltpu.VMEM),
            pl.BlockSpec(memory_space=pl.ANY),
        ],
        out_specs=[pl.BlockSpec(memory_space=pltpu.VMEM)] * axis_size,
        scratch_shapes=[
            pltpu.VMEM((4 * token_count, 128), jnp.bfloat16),
            pltpu.VMEM((mix * token_count, features * mix), jnp.bfloat16),
            pltpu.VMEM((mix * token_count, pairs * head_dim), jnp.float32),
            pltpu.VMEM((token_count, 128), jnp.float32),
            pltpu.VMEM((features // 128, 128), jnp.float32),
            pltpu.VMEM((slots, block, pairs, mix, head_dim), jnp.bfloat16),
            pltpu.SemaphoreType.DMA((slots,)),
        ],
        out_shape=[
            jax.ShapeDtypeStruct((groups, rows, width), jnp.bfloat16 if s else jnp.float32)
            for s in range(axis_size)
        ],
        compiler_params=pltpu.CompilerParams(vmem_limit_bytes=48 * 2**20),
        cost_estimate=pl.CostEstimate(
            flops=2 * qkv_weight.size * token_count,
            bytes_accessed=qkv_weight.size * 2,
            transcendentals=0,
        ),
        name="project",
    )(index, tokens, norm_gain.reshape(-1, 128), weight)


SMEM = pl.BlockSpec(memory_space=pltpu.SMEM)
VMEM = pl.BlockSpec(memory_space=pltpu.VMEM)


def wrap(place, count):
    return lax.rem(place, count)


def finish_kernel(
    width_devices, head_devices, token_size, head_dim, index_ref, cosine_ref, sine_ref, *rest
):
    parts, rest = rest[:width_devices], rest[width_devices:]
    outs, (turned_ref, piece_ref) = rest[:head_devices], rest[head_devices:]
    groups, rows, width = parts[0].shape
    heads = width // head_dim - 1
    group_size = heads - 2
    pad = (piece_ref.shape[0] - group_size * token_size) // 2

    def added(g, lane):
        total = parts[0][g, :, lane : lane + head_dim]
        for part in parts[1:]:
            total = total + part[g, :, lane : lane + head_dim].astype(jnp.float32)
        return total

    squares = jnp.sum(added(0, heads * head_dim), axis=1, keepdims=True)
    inv_rms = lax.rsqrt(squares / D + norm_eps)
    start = pl.multiple_of(index_ref[0] * rows, rows)
    cosine = cosine_ref[pl.ds(start, rows), :]
    sine = sine_ref[pl.ds(start, rows), :]
    for g in range(groups):
        for head in range(heads):
            value = added(g, head * head_dim) * inv_rms
            if head <= group_size:
                value = value * cosine + pltpu.roll(value, head_dim // 2, 1) * sine
            turned_ref[g, head] = value.reshape(head_devices, token_size, head_dim)
    piece_ref[...] = jnp.zeros_like(piece_ref)
    for shift in range(head_devices):
        owner = wrap(index_ref[1] + shift, head_devices)
        for g in range(groups):
            for head in range(heads):
                at = head * token_size
                if head >= group_size:
                    at = group_size * token_size + (head - group_size) * pad
                piece_ref[at : at + token_size, :] = turned_ref[g, head, owner]
            outs[shift][g] = piece_ref[...].astype(jnp.bfloat16)


def finish(parts, cosine, sine, index, head_devices, token_size, head_dim):
    groups, rows, width = parts[0].shape
    heads = width // head_dim - 1
    piece_rows = (heads - 2) * token_size + 2 * (-(-token_size // 16) * 16)
    return pl.pallas_call(
        functools.partial(finish_kernel, len(parts), head_devices, token_size, head_dim),
        in_specs=[SMEM] + [VMEM] * (2 + len(parts)),
        out_specs=[VMEM] * head_devices,
        out_shape=[jax.ShapeDtypeStruct((groups, piece_rows, head_dim), jnp.bfloat16)]
        * head_devices,
        scratch_shapes=[
            pltpu.VMEM((groups, heads, head_devices, token_size, head_dim), jnp.float32),
            pltpu.VMEM((piece_rows, head_dim), jnp.float32),
        ],
        compiler_params=pltpu.CompilerParams(vmem_limit_bytes=SMALL_LIMIT),
        name="finish",
    )(index, cosine, sine, *parts)


def attend_kernel(head_devices, query_rows, index_ref, length_ref, cache_ref, *rest):
    pieces, outs = rest[:head_devices], rest[head_devices:]
    groups, piece_rows, head_dim = pieces[0].shape
    rows_local, _, _, slots, _ = cache_ref.shape
    pad = (piece_rows - query_rows) // 2
    token_size = 2 * rows_local
    scale = 1.0 / math.sqrt(head_dim)
    token_old = lax.rem(lax.broadcasted_iota(jnp.int32, (query_rows, slots), 0), token_size)
    slot = lax.broadcasted_iota(jnp.int32, (query_rows, slots), 1)
    length = jnp.zeros((query_rows, slots), jnp.int32)
    for r in range(rows_local):
        length = jnp.where(token_old // 2 == r, length_ref[r], length)
    visible = slot < length
    token = lax.rem(lax.broadcasted_iota(jnp.int32, (query_rows, pad), 0), token_size)
    other = lax.broadcasted_iota(jnp.int32, (query_rows, pad), 1)
    causal = (other // 2 == token // 2) & (other <= token)
    row_out = lax.rem(lax.broadcasted_iota(jnp.int32, (query_rows, head_dim), 0), token_size) // 2
    last = (((1,), (1,)), ((), ()))
    for shift in range(head_devices):
        source = wrap(index_ref[1] + head_devices - shift, head_devices)
        for g in range(groups):
            group = source * groups + g
            queries = pieces[shift][g, :query_rows, :]
            key_new = pieces[shift][g, query_rows : query_rows + pad, :]
            value_new = pieces[shift][g, query_rows + pad :, :]
            old = None
            for r in range(rows_local):
                term = lax.dot_general(
                    queries, cache_ref[r, 0, group], last, preferred_element_type=jnp.float32
                )
                old = term if old is None else jnp.where(token_old // 2 == r, term, old)
            old = jnp.where(visible, old * scale, -1e30)
            new = lax.dot_general(queries, key_new, last, preferred_element_type=jnp.float32)
            new = jnp.where(causal, new * scale, -1e30)
            highest = jnp.maximum(
                jnp.max(old, axis=1, keepdims=True), jnp.max(new, axis=1, keepdims=True)
            )
            old = jnp.exp(old - highest)
            new = jnp.exp(new - highest)
            total = jnp.sum(old, axis=1, keepdims=True) + jnp.sum(new, axis=1, keepdims=True)
            old = (old / total).astype(jnp.bfloat16)
            new = (new / total).astype(jnp.bfloat16)
            attended = None
            for r in range(rows_local):
                term = jnp.dot(old, cache_ref[r, 1, group], preferred_element_type=jnp.float32)
                attended = term if attended is None else jnp.where(row_out == r, term, attended)
            attended = attended + jnp.dot(new, value_new, preferred_element_type=jnp.float32)
            outs[shift][g] = attended.astype(jnp.bfloat16)


def attend(pieces, cache, lengths, index, query_rows):
    groups, _, head_dim = pieces[0].shape
    return pl.pallas_call(
        functools.partial(attend_kernel, len(pieces), query_rows),
        in_specs=[SMEM, SMEM] + [VMEM] * (1 + len(pieces)),
        out_specs=[VMEM] * len(pieces),
        out_shape=[jax.ShapeDtypeStruct((groups, query_rows, head_dim), jnp.bfloat16)]
        * len(pieces),
        compiler_params=pltpu.CompilerParams(vmem_limit_bytes=SMALL_LIMIT),
        name="attend",
    )(index, lengths, cache, *pieces)


def gather_kernel(token_size, index_ref, *rest):
    pieces, (out_ref, block_ref) = rest[:-2], rest[-2:]
    count = len(pieces)
    groups, query_rows, head_dim = pieces[0].shape
    heads = query_rows // token_size
    for shift in range(count):
        source = wrap(index_ref[1] + shift, count)
        for g in range(groups):
            wide = pieces[shift][g].astype(jnp.float32)
            for head in range(heads):
                lane = (g * heads + head) * head_dim
                block_ref[source, :, lane : lane + head_dim] = wide[
                    head * token_size : (head + 1) * token_size, :
                ]
    for lane in range(0, groups * heads * head_dim, head_dim):
        part = block_ref[:, :, lane : lane + head_dim].reshape(count * token_size, head_dim)
        out_ref[:, lane : lane + head_dim] = part.astype(jnp.bfloat16)


def gather(pieces, index, token_size):
    groups, query_rows, head_dim = pieces[0].shape
    width = groups * (query_rows // token_size) * head_dim
    return pl.pallas_call(
        functools.partial(gather_kernel, token_size),
        in_specs=[SMEM] + [VMEM] * len(pieces),
        out_specs=VMEM,
        out_shape=jax.ShapeDtypeStruct((len(pieces) * token_size, width), jnp.bfloat16),
        scratch_shapes=[pltpu.VMEM((len(pieces), token_size, width), jnp.float32)],
        compiler_params=pltpu.CompilerParams(vmem_limit_bytes=SMALL_LIMIT),
        name="gather",
    )(index, *pieces)


def outward_kernel(block_count, axis_size, index_ref, *rest):
    blocks, weight_ref, rest = rest[:block_count], rest[block_count], rest[block_count + 1 :]
    outs, (left_ref, total_ref) = rest[:axis_size], rest[axis_size:]
    token_count, depth = left_ref.shape
    size = token_count // block_count

    @pl.when(pl.program_id(0) == 0)
    def _():
        for shift in range(block_count):
            source = wrap(index_ref[0] + block_count - shift, block_count)
            left_ref[pl.ds(pl.multiple_of(source * size, size), size), :] = blocks[shift][...]

    rows = token_count // axis_size
    step = pick_block(depth)
    for k in range(0, depth, step):
        term = jnp.dot(
            left_ref[:, k : k + step],
            weight_ref[k : k + step, :],
            preferred_element_type=jnp.float32,
        )
        if k == 0:
            total_ref[...] = term
        else:
            total_ref[...] += term
    for shift in range(axis_size):
        first = pl.multiple_of(wrap(index_ref[1] + shift, axis_size) * rows, rows)
        outs[shift][...] = total_ref[pl.ds(first, rows), :].astype(outs[shift].dtype)


def outward(blocks, weight, axis_size, index):
    size, depth = blocks[0].shape
    token_count = size * len(blocks)
    width = weight.shape[1]
    block = pick_block(width)
    rows = token_count // axis_size
    return pl.pallas_call(
        functools.partial(outward_kernel, len(blocks), axis_size),
        grid=(width // block,),
        in_specs=[SMEM]
        + [VMEM] * len(blocks)
        + [pl.BlockSpec((depth, block), lambda j: (0, j))],
        out_specs=[pl.BlockSpec((rows, block), lambda j: (0, j))] * axis_size,
        scratch_shapes=[
            pltpu.VMEM((token_count, depth), jnp.bfloat16),
            pltpu.VMEM((token_count, block), jnp.float32),
        ],
        out_shape=[
            jax.ShapeDtypeStruct((rows, width), jnp.bfloat16 if s else jnp.float32)
            for s in range(axis_size)
        ],
        compiler_params=pltpu.CompilerParams(vmem_limit_bytes=48 * 2**20),
        cost_estimate=pl.CostEstimate(
            flops=2 * weight.size * token_count,
            bytes_accessed=weight.size * 2,
            transcendentals=0,
        ),
        name="outward",
    )(index, *blocks, weight)


def close_kernel(index_ref, tokens_ref, *rest):
    parts, out_ref = rest[:-1], rest[-1]
    rows, tokens, _ = out_ref.shape
    lanes = 128
    width = parts[0].shape[1]
    for lane in range(0, out_ref.shape[2], lanes):
        column, at = lane // width, lane % width
        total = None
        for part in parts[column * len(parts) * width // out_ref.shape[2] :][
            : len(parts) * width // out_ref.shape[2]
        ]:
            term = part[:, at : at + lanes].astype(jnp.float32)
            total = term if total is None else total + term
        residual = tokens_ref[:, :, lane : lane + lanes].astype(jnp.float32)
        out_ref[:, :, lane : lane + lanes] = residual + total.reshape(rows, tokens, lanes)


def close(tokens, parts, head_devices, index):
    rows = tokens.shape[0] // head_devices
    shape = (rows,) + tokens.shape[1:]
    return pl.pallas_call(
        close_kernel,
        grid_spec=pltpu.PrefetchScalarGridSpec(
            num_scalar_prefetch=1,
            grid=(1,),
            in_specs=[pl.BlockSpec(shape, lambda i, index: (index[1], 0, 0))]
            + [pl.BlockSpec(part.shape, lambda i, index: (0, 0)) for part in parts],
            out_specs=pl.BlockSpec(shape, lambda i, index: (0, 0, 0)),
        ),
        out_shape=jax.ShapeDtypeStruct(shape, jnp.float32),
        compiler_params=pltpu.CompilerParams(vmem_limit_bytes=SMALL_LIMIT),
        name="close",
    )(index, tokens, *parts)


def exchange(pieces, axis, sign=1):
    count = len(pieces)
    return [pieces[0]] + [
        lax.ppermute(pieces[s], axis, shift_pairs(count, sign * s)) for s in range(1, count)
    ]


def body(tokens, norm_gain, qkv_weight, out_weight, kv_cache, lengths, positions):
    rows_local = kv_cache.shape[0]
    width_devices = lax.axis_size("gx")
    head_devices = lax.axis_size("gy")
    index = jnp.stack([lax.axis_index("gx"), lax.axis_index("gy")])
    local_width = tokens.shape[2]
    head_dim = qkv_weight.shape[3]
    group_size = qkv_weight.shape[2] - 2
    token_size = rows_local * 2

    half = head_dim // 2
    frequency = rope_base ** (-2.0 * jnp.arange(half, dtype=jnp.float32) / head_dim)
    places = (positions[:, None] + jnp.arange(2, dtype=jnp.int32)[None, :]).astype(jnp.float32)
    angles = places.reshape(-1, 1) * frequency
    cosine = jnp.cos(angles)
    sine = jnp.sin(angles)
    cosine = jnp.concatenate([cosine, cosine], axis=1)
    sine = jnp.concatenate([-sine, sine], axis=1)
    cache = jnp.transpose(kv_cache, (0, 2, 3, 1, 4))

    parts = project(tokens, norm_gain, qkv_weight, width_devices, index)
    parts = exchange(parts, "gx")
    pieces = finish(parts, cosine, sine, index, head_devices, token_size, head_dim)
    pieces = exchange(pieces, "gy")
    attended = attend(pieces, cache, lengths, index, group_size * token_size)
    attended = exchange(attended, "gy", -1)
    block = gather(attended, index, token_size)
    blocks = exchange([block] * width_devices, "gx")
    out_flat = out_weight.reshape(-1, local_width)
    sums = outward(blocks, out_flat, head_devices, index)
    return close(tokens, exchange(sums, "gy"), head_devices, index)


def solution(mesh):
    return jax.shard_map(
        body,
        mesh=mesh,
        in_specs=(
            P("groups", None, "gx"),
            P("gx"),
            P("gx", "gy", None, None),
            P("gy", None, "gx"),
            P(("groups", "gx", "gy"), None, None, None, None),
            P(("groups", "gx", "gy")),
            P("groups"),
        ),
        out_specs=P(("groups", "gy"), None, "gx"),
        check_vma=False,
    )
```

```python
import functools
import math

import jax
import jax.numpy as jnp
from jax import lax
from jax.experimental import pallas as pl
from jax.experimental.pallas import tpu as pltpu
from jax.sharding import PartitionSpec as P

D = 16384


norm_eps = 1e-05
rope_base = 500000.0
PROJECT_BLOCK = 512
PROJECT_SLOTS = 3
SMALL_LIMIT = 12 * 2**20
OUTWARD_SHARE = 8
OUTWARD_STEP = 512
OUTWARD_SLOTS = 6
OUTWARD_LIMIT = 20 * 2**20
HELD_SHARES = (4, 4, 6)
PAIR_GROUP = 4


def shift_pairs(count, shift):
    return [(i, (i + shift) % count) for i in range(count)]


def in_hbm(array):
    return pltpu.with_memory_space_constraint(array, pltpu.HBM)


def split_squares(total, lanes):
    high = total.astype(jnp.bfloat16).astype(jnp.float32)
    middle = (total - high).astype(jnp.bfloat16).astype(jnp.float32)
    low = total - high - middle
    lane = lax.broadcasted_iota(jnp.int32, (total.shape[0], lanes), 1)
    return jnp.where(
        lane == 0, high, jnp.where(lane == 1, middle, jnp.where(lane == 2, low, 0.0))
    )


def project_kernel(axis_size, block, slots, index_ref, tokens_hbm, gain_hbm, weight_ref, *rest):
    outs, rest = rest[:axis_size], rest[axis_size:]
    (
        hidden_ref,
        spread_ref,
        total_ref,
        sum_ref,
        gain_wide,
        tokens_ref,
        gain_ref,
        buffer,
        arrived,
    ) = rest
    total_rows, pair_rows, features = tokens_ref.shape
    token_count = total_rows * pair_rows
    pairs, mix, head_dim = weight_ref.shape[1:]
    groups = mix // 2
    steps = features // block
    lanes = 128

    def fetch(step, slot):
        return pltpu.make_async_copy(
            weight_ref.at[pl.ds(step * block, block)], buffer.at[slot], arrived.at[slot]
        )

    early = [
        pltpu.make_async_copy(tokens_hbm, tokens_ref, arrived.at[slots]),
        pltpu.make_async_copy(gain_hbm, gain_ref, arrived.at[slots + 1]),
    ]
    for copy in early:
        copy.start()
    for step in range(min(slots, steps)):
        fetch(step, step).start()

    wide = lanes * mix
    place = lax.broadcasted_iota(jnp.int32, (lanes, wide), 0)
    column = lax.broadcasted_iota(jnp.int32, (lanes, wide), 1)
    repeat = (column // mix == place).astype(jnp.bfloat16)
    member_of = lax.rem(lax.broadcasted_iota(jnp.int32, (token_count, wide), 1), mix)
    members = [(member_of == m).astype(jnp.bfloat16) for m in range(mix)]
    for copy in early:
        copy.wait()
    gain_wide[...] = gain_ref[...].astype(jnp.float32)
    squares = jnp.zeros((token_count, lanes), jnp.float32)
    group = 4
    for i in range(0, features // lanes, group):
        for j in range(group):
            at = (i + j) * lanes
            piece = tokens_ref[:, :, at : at + lanes].reshape(token_count, lanes)
            piece = piece.astype(jnp.float32)
            squares = squares + piece * piece
            hidden_ref[j * token_count : (j + 1) * token_count, :] = (
                piece * gain_wide[i + j : i + j + 1, :]
            ).astype(jnp.bfloat16)
        repeated = jnp.dot(hidden_ref[...], repeat, preferred_element_type=jnp.float32)
        repeated = repeated.astype(jnp.bfloat16)
        for j in range(group):
            for m in range(mix):
                spread_ref[
                    m * token_count : (m + 1) * token_count, (i + j) * wide : (i + j + 1) * wide
                ] = repeated[j * token_count : (j + 1) * token_count, :] * members[m]
    total_ref[...] = jnp.zeros_like(total_ref)

    @pl.loop(0, steps)
    def _(step):
        slot = lax.rem(step, slots)
        fetch(step, slot).wait()
        left = spread_ref.at[:, pl.ds(pl.multiple_of(step * block * mix, 128), block * mix)]
        for first in range(0, pairs, PAIR_GROUP):
            count = min(PAIR_GROUP, pairs - first)
            weights = [
                buffer[slot, :, first + i].reshape(block * mix, head_dim) for i in range(count)
            ]
            weights = jnp.concatenate(weights, axis=1) if count > 1 else weights[0]
            total_ref[:, first * head_dim : (first + count) * head_dim] += jnp.dot(
                left[...], weights, preferred_element_type=jnp.float32
            )

        @pl.when(step + slots < steps)
        def _():
            fetch(step + slots, slot).start()

    rows = token_count // axis_size
    sum_ref[...] = split_squares(jnp.sum(squares, axis=1, keepdims=True), lanes)
    for shift in range(axis_size):
        owner = lax.rem(index_ref[0] + shift, axis_size)
        first = pl.multiple_of(owner * rows, rows)
        own = outs[shift]
        for g in range(groups):
            for head in range(2 * pairs):
                start = ((head % 2) * groups + g) * token_count
                lane = (head // 2) * head_dim
                own[g, :, head * head_dim : (head + 1) * head_dim] = total_ref[
                    pl.ds(start + first, rows), lane : lane + head_dim
                ].astype(own.dtype)
            own[g, :, 2 * pairs * head_dim :] = sum_ref[pl.ds(first, rows), :].astype(own.dtype)


def project(tokens, norm_gain, qkv_weight, axis_size, index):
    features, groups, heads, head_dim = qkv_weight.shape
    token_count = tokens.shape[0] * tokens.shape[1]
    mix = 2 * groups
    pairs = heads // 2
    block = min(features, PROJECT_BLOCK)
    slots = PROJECT_SLOTS
    rows = token_count // axis_size
    width = heads * head_dim + 128
    weight = jnp.transpose(qkv_weight, (0, 2, 1, 3)).reshape(features, pairs, mix, head_dim)
    return pl.pallas_call(
        functools.partial(project_kernel, axis_size, block, slots),
        in_specs=[
            pl.BlockSpec(memory_space=pltpu.SMEM),
            pl.BlockSpec(memory_space=pltpu.HBM),
            pl.BlockSpec(memory_space=pltpu.HBM),
            pl.BlockSpec(memory_space=pltpu.HBM),
        ],
        out_specs=[pl.BlockSpec(memory_space=pltpu.VMEM)] * axis_size,
        scratch_shapes=[
            pltpu.VMEM((4 * token_count, 128), jnp.bfloat16),
            pltpu.VMEM((mix * token_count, features * mix), jnp.bfloat16),
            pltpu.VMEM((mix * token_count, pairs * head_dim), jnp.float32),
            pltpu.VMEM((token_count, 128), jnp.float32),
            pltpu.VMEM((features // 128, 128), jnp.float32),
            pltpu.VMEM(tokens.shape, tokens.dtype),
            pltpu.VMEM((features // 128, 128), norm_gain.dtype),
            pltpu.VMEM((slots, block, pairs, mix, head_dim), jnp.bfloat16),
            pltpu.SemaphoreType.DMA((slots + 2,)),
        ],
        out_shape=[
            jax.ShapeDtypeStruct((groups, rows, width), jnp.bfloat16 if s else jnp.float32)
            for s in range(axis_size)
        ],
        compiler_params=pltpu.CompilerParams(vmem_limit_bytes=48 * 2**20),
        cost_estimate=pl.CostEstimate(
            flops=2 * qkv_weight.size * token_count,
            bytes_accessed=qkv_weight.size * 2,
            transcendentals=0,
        ),
        name="project",
    )(index, *[in_hbm(array) for array in (tokens, norm_gain.reshape(-1, 128), weight)])


SMEM = pl.BlockSpec(memory_space=pltpu.SMEM)
VMEM = pl.BlockSpec(memory_space=pltpu.VMEM)


def wrap(place, count):
    return lax.rem(place, count)


def finish_kernel(
    width_devices, head_devices, token_size, head_dim, index_ref, _, cosine_ref, sine_ref, *rest
):
    parts, rest = rest[:width_devices], rest[width_devices:]
    outs, (turned_ref, piece_ref) = rest[:head_devices], rest[head_devices:]
    groups, rows, width = parts[0].shape
    heads = width // head_dim - 1
    group_size = heads - 2
    pad = (piece_ref.shape[0] - group_size * token_size) // 2

    def added(g, lane):
        total = parts[0][g, :, lane : lane + head_dim]
        for part in parts[1:]:
            total = total + part[g, :, lane : lane + head_dim].astype(jnp.float32)
        return total

    squares = jnp.sum(added(0, heads * head_dim), axis=1, keepdims=True)
    inv_rms = lax.rsqrt(squares / D + norm_eps)
    start = pl.multiple_of(index_ref[0] * rows, rows)
    cosine = cosine_ref[pl.ds(start, rows), :]
    sine = sine_ref[pl.ds(start, rows), :]
    for g in range(groups):
        for head in range(heads):
            value = added(g, head * head_dim) * inv_rms
            if head <= group_size:
                value = value * cosine + pltpu.roll(value, head_dim // 2, 1) * sine
            turned_ref[g, head] = value.reshape(head_devices, token_size, head_dim)
    piece_ref[...] = jnp.zeros_like(piece_ref)
    for shift in range(head_devices):
        owner = wrap(index_ref[1] + shift, head_devices)
        for g in range(groups):
            for head in range(heads):
                at = head * token_size
                if head >= group_size:
                    at = group_size * token_size + (head - group_size) * pad
                piece_ref[at : at + token_size, :] = turned_ref[g, head, owner]
            outs[shift][g] = piece_ref[...].astype(jnp.bfloat16)


def finish(parts, cosine, sine, early, index, head_devices, token_size, head_dim):
    groups, rows, width = parts[0].shape
    heads = width // head_dim - 1
    piece_rows = (heads - 2) * token_size + 2 * (-(-token_size // 16) * 16)
    return pl.pallas_call(
        functools.partial(finish_kernel, len(parts), head_devices, token_size, head_dim),
        in_specs=[SMEM, pl.BlockSpec(memory_space=pl.ANY)] + [VMEM] * (2 + len(parts)),
        out_specs=[VMEM] * head_devices,
        out_shape=[jax.ShapeDtypeStruct((groups, piece_rows, head_dim), jnp.bfloat16)]
        * head_devices,
        scratch_shapes=[
            pltpu.VMEM((groups, heads, head_devices, token_size, head_dim), jnp.float32),
            pltpu.VMEM((piece_rows, head_dim), jnp.float32),
        ],
        compiler_params=pltpu.CompilerParams(vmem_limit_bytes=SMALL_LIMIT),
        name="finish",
    )(index, early, cosine, sine, *parts)


def attend_kernel(head_devices, query_rows, index_ref, length_ref, cache_ref, *rest):
    pieces, rest = rest[:head_devices], rest[head_devices:]
    outs, rest = rest[:head_devices], rest[head_devices:]
    old_ref, new_ref, old_weight_ref, new_weight_ref = rest
    groups, piece_rows, head_dim = pieces[0].shape
    rows_local, _, _, slots, _ = cache_ref.shape
    pad = (piece_rows - query_rows) // 2
    token_size = 2 * rows_local
    scale = 1.0 / math.sqrt(head_dim)
    token_old = lax.rem(lax.broadcasted_iota(jnp.int32, (query_rows, slots), 0), token_size)
    slot = lax.broadcasted_iota(jnp.int32, (query_rows, slots), 1)
    length = jnp.zeros((query_rows, slots), jnp.int32)
    for r in range(rows_local):
        length = jnp.where(token_old // 2 == r, length_ref[r], length)
    visible = slot < length
    token = lax.rem(lax.broadcasted_iota(jnp.int32, (query_rows, pad), 0), token_size)
    other = lax.broadcasted_iota(jnp.int32, (query_rows, pad), 1)
    causal = (other // 2 == token // 2) & (other <= token)
    row_out = lax.rem(lax.broadcasted_iota(jnp.int32, (query_rows, head_dim), 0), token_size) // 2
    last = (((1,), (1,)), ((), ()))
    jobs = []
    for shift in range(head_devices):
        source = wrap(index_ref[1] + head_devices - shift, head_devices)
        jobs += [(shift, g, source * groups + g) for g in range(groups)]
    for job, (shift, g, group) in enumerate(jobs):
        queries = pieces[shift][g, :query_rows, :]
        old = None
        for r in range(rows_local):
            term = lax.dot_general(
                queries, cache_ref[r, 0, group], last, preferred_element_type=jnp.float32
            )
            old = term if old is None else jnp.where(token_old // 2 == r, term, old)
        old_ref[job] = jnp.where(visible, old * scale, -1e30)
        key_new = pieces[shift][g, query_rows : query_rows + pad, :]
        new = lax.dot_general(queries, key_new, last, preferred_element_type=jnp.float32)
        new_ref[job] = jnp.where(causal, new * scale, -1e30)
    old = old_ref[...]
    new = new_ref[...]
    highest = jnp.maximum(
        jnp.max(old, axis=2, keepdims=True), jnp.max(new, axis=2, keepdims=True)
    )
    old = jnp.exp(old - highest)
    new = jnp.exp(new - highest)
    total = jnp.sum(old, axis=2, keepdims=True) + jnp.sum(new, axis=2, keepdims=True)
    inverse = 1.0 / total
    old_weight_ref[...] = (old * inverse).astype(jnp.bfloat16)
    new_weight_ref[...] = (new * inverse).astype(jnp.bfloat16)
    for job, (shift, g, group) in enumerate(jobs):
        attended = None
        for r in range(rows_local):
            term = jnp.dot(
                old_weight_ref[job], cache_ref[r, 1, group], preferred_element_type=jnp.float32
            )
            attended = term if attended is None else jnp.where(row_out == r, term, attended)
        value_new = pieces[shift][g, query_rows + pad :, :]
        attended = attended + jnp.dot(
            new_weight_ref[job], value_new, preferred_element_type=jnp.float32
        )
        outs[shift][g] = attended.astype(jnp.bfloat16)


def attend(pieces, cache, lengths, index, query_rows):
    groups, piece_rows, head_dim = pieces[0].shape
    slots, pad = cache.shape[3], (piece_rows - query_rows) // 2
    return pl.pallas_call(
        functools.partial(attend_kernel, len(pieces), query_rows),
        in_specs=[SMEM, SMEM] + [VMEM] * (1 + len(pieces)),
        out_specs=[VMEM] * len(pieces),
        out_shape=[jax.ShapeDtypeStruct((groups, query_rows, head_dim), jnp.bfloat16)]
        * len(pieces),
        scratch_shapes=[
            pltpu.VMEM((len(pieces) * groups, query_rows, count), kind)
            for kind in (jnp.float32, jnp.bfloat16)
            for count in (slots, pad)
        ],
        compiler_params=pltpu.CompilerParams(vmem_limit_bytes=SMALL_LIMIT),
        name="attend",
    )(index, lengths, cache, *pieces)


def gather_kernel(token_size, index_ref, *rest):
    pieces, (out_ref, block_ref) = rest[:-2], rest[-2:]
    count = len(pieces)
    groups, query_rows, head_dim = pieces[0].shape
    heads = query_rows // token_size
    for shift in range(count):
        source = wrap(index_ref[1] + shift, count)
        for g in range(groups):
            wide = pieces[shift][g].astype(jnp.float32)
            for head in range(heads):
                lane = (g * heads + head) * head_dim
                block_ref[source, :, lane : lane + head_dim] = wide[
                    head * token_size : (head + 1) * token_size, :
                ]
    for lane in range(0, groups * heads * head_dim, head_dim):
        part = block_ref[:, :, lane : lane + head_dim].reshape(count * token_size, head_dim)
        out_ref[:, lane : lane + head_dim] = part.astype(jnp.bfloat16)


def gather(pieces, index, token_size):
    groups, query_rows, head_dim = pieces[0].shape
    width = groups * (query_rows // token_size) * head_dim
    return pl.pallas_call(
        functools.partial(gather_kernel, token_size),
        in_specs=[SMEM] + [VMEM] * len(pieces),
        out_specs=VMEM,
        out_shape=jax.ShapeDtypeStruct((len(pieces) * token_size, width), jnp.bfloat16),
        scratch_shapes=[pltpu.VMEM((len(pieces), token_size, width), jnp.float32)],
        compiler_params=pltpu.CompilerParams(vmem_limit_bytes=SMALL_LIMIT),
        name="gather",
    )(index, *pieces)


def hold_kernel(first, after_ref, through_ref, source_ref, held_ref, same_ref, arrived):
    rows = pl.ds(first, held_ref.shape[0])
    copy = pltpu.make_async_copy(source_ref.at[rows], held_ref, arrived)
    copy.start()
    copy.wait()


def hold(source, first, count, after, through):
    return pl.pallas_call(
        functools.partial(hold_kernel, first),
        in_specs=[pl.BlockSpec(memory_space=space) for space in (pl.ANY, pl.ANY, pltpu.HBM)],
        out_specs=[VMEM, pl.BlockSpec(memory_space=pl.ANY)],
        out_shape=[
            pltpu.VMEM((count, source.shape[1]), source.dtype),
            jax.ShapeDtypeStruct(through.shape, through.dtype),
        ],
        input_output_aliases={1: 1},
        scratch_shapes=[pltpu.SemaphoreType.DMA],
        compiler_params=pltpu.CompilerParams(vmem_limit_bytes=2**20),
        cost_estimate=pl.CostEstimate(
            flops=0, bytes_accessed=count * source.shape[1] * 2, transcendentals=0
        ),
        name="hold",
    )(after, through, in_hbm(source))


def outward_kernel(block_count, axis_size, begin, held_count, index_ref, weight_ref, *rest):
    held, rest = rest[:held_count], rest[held_count:]
    blocks, rest = rest[:block_count], rest[block_count:]
    outs, (left_ref, total_ref, buffer, arrived) = rest[:axis_size], rest[axis_size:]
    token_count, depth = left_ref.shape
    size = token_count // block_count
    slots, step, width = buffer.shape
    kept = sum(part.shape[0] for part in held)
    steps = (depth - kept) // step

    def fetch(k, slot):
        return pltpu.make_async_copy(
            weight_ref.at[pl.ds(kept + k * step, step), pl.ds(begin, width)],
            buffer.at[slot],
            arrived.at[slot],
        )

    for k in range(min(slots, steps)):
        fetch(k, k).start()
    for shift in range(block_count):
        source = wrap(index_ref[0] + block_count - shift, block_count)
        left_ref[pl.ds(pl.multiple_of(source * size, size), size), :] = blocks[shift][...]
    first = 0
    for part in held:
        term = jnp.dot(
            left_ref[:, first : first + part.shape[0]],
            part[:, begin : begin + width],
            preferred_element_type=jnp.float32,
        )
        if first == 0:
            total_ref[...] = term
        else:
            total_ref[...] += term
        first += part.shape[0]

    @pl.loop(0, steps)
    def _(k):
        slot = lax.rem(k, slots)
        fetch(k, slot).wait()
        total_ref[...] += jnp.dot(
            left_ref[:, pl.ds(pl.multiple_of(kept + k * step, step), step)],
            buffer[slot],
            preferred_element_type=jnp.float32,
        )

        @pl.when(k + slots < steps)
        def _():
            fetch(k + slots, slot).start()

    rows = token_count // axis_size
    for shift in range(axis_size):
        first = pl.multiple_of(wrap(index_ref[1] + shift, axis_size) * rows, rows)
        outs[shift][...] = total_ref[pl.ds(first, rows), :].astype(outs[shift].dtype)


def outward(blocks, weight, held, begin, width, axis_size, index):
    size, depth = blocks[0].shape
    token_count = size * len(blocks)
    rows = token_count // axis_size
    step = math.gcd(depth - sum(part.shape[0] for part in held), OUTWARD_STEP)
    return pl.pallas_call(
        functools.partial(outward_kernel, len(blocks), axis_size, begin, len(held)),
        in_specs=[SMEM, pl.BlockSpec(memory_space=pltpu.HBM)] + [VMEM] * (len(held) + len(blocks)),
        out_specs=[VMEM] * axis_size,
        scratch_shapes=[
            pltpu.VMEM((token_count, depth), jnp.bfloat16),
            pltpu.VMEM((token_count, width), jnp.float32),
            pltpu.VMEM((OUTWARD_SLOTS, step, width), weight.dtype),
            pltpu.SemaphoreType.DMA((OUTWARD_SLOTS,)),
        ],
        out_shape=[
            jax.ShapeDtypeStruct((rows, width), jnp.bfloat16 if s else jnp.float32)
            for s in range(axis_size)
        ],
        compiler_params=pltpu.CompilerParams(vmem_limit_bytes=OUTWARD_LIMIT),
        cost_estimate=pl.CostEstimate(
            flops=2 * depth * width * token_count,
            bytes_accessed=2 * depth * width,
            transcendentals=0,
        ),
        name="outward",
    )(
        index,
        in_hbm(weight),
        *[pltpu.with_memory_space_constraint(part, pltpu.VMEM) for part in held],
        *blocks,
    )


def close_kernel(count, index_ref, tokens_ref, *rest):
    parts, out_ref = rest[:-1], rest[-1]
    rows, tokens, _ = out_ref.shape
    lanes = 128
    begin = 0
    for span in range(0, len(parts), count):
        width = parts[span].shape[1]
        for lane in range(0, width, lanes):
            total = parts[span][:, lane : lane + lanes]
            for part in parts[span + 1 : span + count]:
                total = total + part[:, lane : lane + lanes].astype(jnp.float32)
            at = begin + lane
            residual = tokens_ref[:, :, at : at + lanes].astype(jnp.float32)
            out_ref[:, :, at : at + lanes] = residual + total.reshape(rows, tokens, lanes)
        begin += width


def close(tokens, parts, head_devices, index):
    rows = tokens.shape[0] // head_devices
    shape = (rows,) + tokens.shape[1:]
    return pl.pallas_call(
        functools.partial(close_kernel, head_devices),
        grid_spec=pltpu.PrefetchScalarGridSpec(
            num_scalar_prefetch=1,
            grid=(1,),
            in_specs=[pl.BlockSpec(shape, lambda i, index: (index[1], 0, 0))]
            + [pl.BlockSpec(part.shape, lambda i, index: (0, 0)) for part in parts],
            out_specs=pl.BlockSpec(shape, lambda i, index: (0, 0, 0)),
        ),
        out_shape=jax.ShapeDtypeStruct(shape, jnp.float32),
        compiler_params=pltpu.CompilerParams(vmem_limit_bytes=SMALL_LIMIT),
        name="close",
    )(index, tokens, *parts)


def exchange(pieces, axis, sign=1):
    count = len(pieces)
    return [pieces[0]] + [
        lax.ppermute(pieces[s], axis, shift_pairs(count, sign * s)) for s in range(1, count)
    ]


def body(tokens, norm_gain, qkv_weight, out_weight, kv_cache, lengths, positions):
    rows_local = kv_cache.shape[0]
    width_devices = lax.axis_size("gx")
    head_devices = lax.axis_size("gy")
    index = jnp.stack([lax.axis_index("gx"), lax.axis_index("gy")])
    local_width = tokens.shape[2]
    head_dim = qkv_weight.shape[3]
    group_size = qkv_weight.shape[2] - 2
    token_size = rows_local * 2

    half = head_dim // 2
    frequency = rope_base ** (-2.0 * jnp.arange(half, dtype=jnp.float32) / head_dim)
    places = (positions[:, None] + jnp.arange(2, dtype=jnp.int32)[None, :]).astype(jnp.float32)
    angles = places.reshape(-1, 1) * frequency
    cosine = jnp.cos(angles)
    sine = jnp.sin(angles)
    cosine = jnp.concatenate([cosine, cosine], axis=1)
    sine = jnp.concatenate([-sine, sine], axis=1)
    cache = jnp.transpose(kv_cache, (0, 2, 3, 1, 4))

    parts = list(project(tokens, norm_gain, qkv_weight, width_devices, index))
    out_flat = out_weight.reshape(-1, local_width)
    cuts = [0]
    for share in HELD_SHARES:
        cuts.append(cuts[-1] + out_flat.shape[0] * share // 16)
    sizes = [end - begin for begin, end in zip(cuts, cuts[1:])]
    held = []
    parts = exchange(parts, "gx")
    pieces = list(
        finish(parts, cosine, sine, cache, index, head_devices, token_size, head_dim)
    )
    if sizes[0]:
        part, pieces[0] = hold(out_flat, cuts[0], sizes[0], pieces[1], pieces[0])
        held.append(part)
    pieces = exchange(pieces, "gy")
    attended = list(attend(pieces, cache, lengths, index, group_size * token_size))
    if sizes[1]:
        part, attended[0] = hold(out_flat, cuts[1], sizes[1], attended[1], attended[0])
        held.append(part)
    attended = exchange(attended, "gy", -1)
    block = gather(attended, index, token_size)
    part, late = hold(out_flat, cuts[2], sizes[2], block, index + 0)
    held.append(part)
    blocks = exchange([block] * width_devices, "gx")
    cut = local_width * OUTWARD_SHARE // 16 // 128 * 128
    sums = []
    for begin, end in ((0, cut), (cut, local_width)):
        part = outward(blocks, out_flat, held, begin, end - begin, head_devices, late)
        sums += exchange(part, "gy")
    return close(tokens, sums, head_devices, index)


def solution(mesh):
    return jax.shard_map(
        body,
        mesh=mesh,
        in_specs=(
            P("groups", None, "gx"),
            P("gx"),
            P("gx", "gy", None, None),
            P("gy", None, "gx"),
            P(("groups", "gx", "gy"), None, None, None, None),
            P(("groups", "gx", "gy")),
            P("groups"),
        ),
        out_specs=P(("groups", "gy"), None, "gx"),
        check_vma=False,
    )
```

```python
import functools
import math

import jax
import jax.numpy as jnp
from jax import lax
from jax.experimental import pallas as pl
from jax.experimental.pallas import tpu as pltpu
from jax.sharding import PartitionSpec as P

D = 16384


norm_eps = 1e-05
rope_base = 500000.0
PROJECT_BLOCK = 512
PROJECT_SLOTS = 3
SMALL_LIMIT = 12 * 2**20
OUTWARD_SHARE = 8
OUTWARD_STEP = 1024
OUTWARD_LIMIT = 12 * 2**20
HELD_SHARES = (2, 4, 2, 7)
PAIR_GROUP = 4


def shift_pairs(count, shift):
    return [(i, (i + shift) % count) for i in range(count)]


def in_hbm(array):
    return pltpu.with_memory_space_constraint(array, pltpu.HBM)


def split_squares(total, lanes):
    high = total.astype(jnp.bfloat16).astype(jnp.float32)
    middle = (total - high).astype(jnp.bfloat16).astype(jnp.float32)
    low = total - high - middle
    lane = lax.broadcasted_iota(jnp.int32, (total.shape[0], lanes), 1)
    return jnp.where(
        lane == 0, high, jnp.where(lane == 1, middle, jnp.where(lane == 2, low, 0.0))
    )


def project_kernel(axis_size, block, slots, index_ref, tokens_hbm, gain_hbm, weight_ref, *rest):
    outs, rest = rest[:axis_size], rest[axis_size:]
    (
        hidden_ref,
        spread_ref,
        total_ref,
        sum_ref,
        gain_wide,
        tokens_ref,
        gain_ref,
        buffer,
        arrived,
    ) = rest
    total_rows, pair_rows, features = tokens_ref.shape
    token_count = total_rows * pair_rows
    pairs, mix, head_dim = weight_ref.shape[1:]
    groups = mix // 2
    steps = features // block
    lanes = 128

    def fetch(step, slot):
        return pltpu.make_async_copy(
            weight_ref.at[pl.ds(step * block, block)], buffer.at[slot], arrived.at[slot]
        )

    early = [
        pltpu.make_async_copy(tokens_hbm, tokens_ref, arrived.at[slots]),
        pltpu.make_async_copy(gain_hbm, gain_ref, arrived.at[slots + 1]),
    ]
    for copy in early:
        copy.start()
    for step in range(min(slots, steps)):
        fetch(step, step).start()

    wide = lanes * mix
    place = lax.broadcasted_iota(jnp.int32, (lanes, wide), 0)
    column = lax.broadcasted_iota(jnp.int32, (lanes, wide), 1)
    repeat = (column // mix == place).astype(jnp.bfloat16)
    member_of = lax.rem(lax.broadcasted_iota(jnp.int32, (token_count, wide), 1), mix)
    members = [(member_of == m).astype(jnp.bfloat16) for m in range(mix)]
    for copy in early:
        copy.wait()
    gain_wide[...] = gain_ref[...].astype(jnp.float32)
    squares = jnp.zeros((token_count, lanes), jnp.float32)
    group = 4
    for i in range(0, features // lanes, group):
        for j in range(group):
            at = (i + j) * lanes
            piece = tokens_ref[:, :, at : at + lanes].reshape(token_count, lanes)
            piece = piece.astype(jnp.float32)
            squares = squares + piece * piece
            hidden_ref[j * token_count : (j + 1) * token_count, :] = (
                piece * gain_wide[i + j : i + j + 1, :]
            ).astype(jnp.bfloat16)
        repeated = jnp.dot(hidden_ref[...], repeat, preferred_element_type=jnp.float32)
        repeated = repeated.astype(jnp.bfloat16)
        for j in range(group):
            for m in range(mix):
                spread_ref[
                    m * token_count : (m + 1) * token_count, (i + j) * wide : (i + j + 1) * wide
                ] = repeated[j * token_count : (j + 1) * token_count, :] * members[m]
    total_ref[...] = jnp.zeros_like(total_ref)

    @pl.loop(0, steps)
    def _(step):
        slot = lax.rem(step, slots)
        fetch(step, slot).wait()
        left = spread_ref.at[:, pl.ds(pl.multiple_of(step * block * mix, 128), block * mix)]
        for first in range(0, pairs, PAIR_GROUP):
            count = min(PAIR_GROUP, pairs - first)
            weights = [
                buffer[slot, :, first + i].reshape(block * mix, head_dim) for i in range(count)
            ]
            weights = jnp.concatenate(weights, axis=1) if count > 1 else weights[0]
            total_ref[:, first * head_dim : (first + count) * head_dim] += jnp.dot(
                left[...], weights, preferred_element_type=jnp.float32
            )

        @pl.when(step + slots < steps)
        def _():
            fetch(step + slots, slot).start()

    rows = token_count // axis_size
    sum_ref[...] = split_squares(jnp.sum(squares, axis=1, keepdims=True), lanes)
    for shift in range(axis_size):
        owner = lax.rem(index_ref[0] + shift, axis_size)
        first = pl.multiple_of(owner * rows, rows)
        own = outs[shift]
        for g in range(groups):
            for head in range(2 * pairs):
                start = ((head % 2) * groups + g) * token_count
                lane = (head // 2) * head_dim
                own[g, :, head * head_dim : (head + 1) * head_dim] = total_ref[
                    pl.ds(start + first, rows), lane : lane + head_dim
                ].astype(own.dtype)
            own[g, :, 2 * pairs * head_dim :] = sum_ref[pl.ds(first, rows), :].astype(own.dtype)


def project(tokens, norm_gain, qkv_weight, axis_size, index):
    features, groups, heads, head_dim = qkv_weight.shape
    token_count = tokens.shape[0] * tokens.shape[1]
    mix = 2 * groups
    pairs = heads // 2
    block = min(features, PROJECT_BLOCK)
    slots = PROJECT_SLOTS
    rows = token_count // axis_size
    width = heads * head_dim + 128
    weight = jnp.transpose(qkv_weight, (0, 2, 1, 3)).reshape(features, pairs, mix, head_dim)
    return pl.pallas_call(
        functools.partial(project_kernel, axis_size, block, slots),
        in_specs=[
            pl.BlockSpec(memory_space=pltpu.SMEM),
            pl.BlockSpec(memory_space=pltpu.HBM),
            pl.BlockSpec(memory_space=pltpu.HBM),
            pl.BlockSpec(memory_space=pltpu.HBM),
        ],
        out_specs=[pl.BlockSpec(memory_space=pltpu.VMEM)] * axis_size,
        scratch_shapes=[
            pltpu.VMEM((4 * token_count, 128), jnp.bfloat16),
            pltpu.VMEM((mix * token_count, features * mix), jnp.bfloat16),
            pltpu.VMEM((mix * token_count, pairs * head_dim), jnp.float32),
            pltpu.VMEM((token_count, 128), jnp.float32),
            pltpu.VMEM((features // 128, 128), jnp.float32),
            pltpu.VMEM(tokens.shape, tokens.dtype),
            pltpu.VMEM((features // 128, 128), norm_gain.dtype),
            pltpu.VMEM((slots, block, pairs, mix, head_dim), jnp.bfloat16),
            pltpu.SemaphoreType.DMA((slots + 2,)),
        ],
        out_shape=[
            jax.ShapeDtypeStruct((groups, rows, width), jnp.bfloat16 if s else jnp.float32)
            for s in range(axis_size)
        ],
        compiler_params=pltpu.CompilerParams(vmem_limit_bytes=48 * 2**20),
        cost_estimate=pl.CostEstimate(
            flops=2 * qkv_weight.size * token_count,
            bytes_accessed=qkv_weight.size * 2,
            transcendentals=0,
        ),
        name="project",
    )(index, *[in_hbm(array) for array in (tokens, norm_gain.reshape(-1, 128), weight)])


SMEM = pl.BlockSpec(memory_space=pltpu.SMEM)
VMEM = pl.BlockSpec(memory_space=pltpu.VMEM)


def wrap(place, count):
    return lax.rem(place, count)


def finish_kernel(
    width_devices, head_devices, token_size, head_dim, index_ref, _, cosine_ref, sine_ref, *rest
):
    parts, rest = rest[:width_devices], rest[width_devices:]
    outs, (turned_ref, piece_ref) = rest[:head_devices], rest[head_devices:]
    groups, rows, width = parts[0].shape
    heads = width // head_dim - 1
    group_size = heads - 2
    pad = (piece_ref.shape[0] - group_size * token_size) // 2

    def added(g, lane):
        total = parts[0][g, :, lane : lane + head_dim]
        for part in parts[1:]:
            total = total + part[g, :, lane : lane + head_dim].astype(jnp.float32)
        return total

    squares = jnp.sum(added(0, heads * head_dim), axis=1, keepdims=True)
    inv_rms = lax.rsqrt(squares / D + norm_eps)
    start = pl.multiple_of(index_ref[0] * rows, rows)
    cosine = cosine_ref[pl.ds(start, rows), :]
    sine = sine_ref[pl.ds(start, rows), :]
    for g in range(groups):
        for head in range(heads):
            value = added(g, head * head_dim) * inv_rms
            if head <= group_size:
                value = value * cosine + pltpu.roll(value, head_dim // 2, 1) * sine
            turned_ref[g, head] = value.reshape(head_devices, token_size, head_dim)
    piece_ref[...] = jnp.zeros_like(piece_ref)
    for shift in range(head_devices):
        owner = wrap(index_ref[1] + shift, head_devices)
        for g in range(groups):
            for head in range(heads):
                at = head * token_size
                if head >= group_size:
                    at = group_size * token_size + (head - group_size) * pad
                piece_ref[at : at + token_size, :] = turned_ref[g, head, owner]
            outs[shift][g] = piece_ref[...].astype(jnp.bfloat16)


def finish(parts, cosine, sine, early, index, head_devices, token_size, head_dim):
    groups, rows, width = parts[0].shape
    heads = width // head_dim - 1
    piece_rows = (heads - 2) * token_size + 2 * (-(-token_size // 16) * 16)
    return pl.pallas_call(
        functools.partial(finish_kernel, len(parts), head_devices, token_size, head_dim),
        in_specs=[SMEM, pl.BlockSpec(memory_space=pl.ANY)] + [VMEM] * (2 + len(parts)),
        out_specs=[VMEM] * head_devices,
        out_shape=[jax.ShapeDtypeStruct((groups, piece_rows, head_dim), jnp.bfloat16)]
        * head_devices,
        scratch_shapes=[
            pltpu.VMEM((groups, heads, head_devices, token_size, head_dim), jnp.float32),
            pltpu.VMEM((piece_rows, head_dim), jnp.float32),
        ],
        compiler_params=pltpu.CompilerParams(vmem_limit_bytes=SMALL_LIMIT),
        name="finish",
    )(index, early, cosine, sine, *parts)


def attend_kernel(head_devices, query_rows, index_ref, length_ref, cache_ref, *rest):
    pieces, rest = rest[:head_devices], rest[head_devices:]
    outs, rest = rest[:head_devices], rest[head_devices:]
    old_ref, new_ref, old_weight_ref, new_weight_ref = rest
    groups, piece_rows, head_dim = pieces[0].shape
    rows_local, _, _, slots, _ = cache_ref.shape
    pad = (piece_rows - query_rows) // 2
    token_size = 2 * rows_local
    scale = 1.0 / math.sqrt(head_dim)
    token_old = lax.rem(lax.broadcasted_iota(jnp.int32, (query_rows, slots), 0), token_size)
    slot = lax.broadcasted_iota(jnp.int32, (query_rows, slots), 1)
    length = jnp.zeros((query_rows, slots), jnp.int32)
    for r in range(rows_local):
        length = jnp.where(token_old // 2 == r, length_ref[r], length)
    visible = slot < length
    token = lax.rem(lax.broadcasted_iota(jnp.int32, (query_rows, pad), 0), token_size)
    other = lax.broadcasted_iota(jnp.int32, (query_rows, pad), 1)
    causal = (other // 2 == token // 2) & (other <= token)
    row_out = lax.rem(lax.broadcasted_iota(jnp.int32, (query_rows, head_dim), 0), token_size) // 2
    last = (((1,), (1,)), ((), ()))
    jobs = []
    for shift in range(head_devices):
        source = wrap(index_ref[1] + head_devices - shift, head_devices)
        jobs += [(shift, g, source * groups + g) for g in range(groups)]
    for job, (shift, g, group) in enumerate(jobs):
        queries = pieces[shift][g, :query_rows, :]
        old = None
        for r in range(rows_local):
            term = lax.dot_general(
                queries, cache_ref[r, 0, group], last, preferred_element_type=jnp.float32
            )
            old = term if old is None else jnp.where(token_old // 2 == r, term, old)
        old_ref[job] = jnp.where(visible, old * scale, -1e30)
        key_new = pieces[shift][g, query_rows : query_rows + pad, :]
        new = lax.dot_general(queries, key_new, last, preferred_element_type=jnp.float32)
        new_ref[job] = jnp.where(causal, new * scale, -1e30)
    old = old_ref[...]
    new = new_ref[...]
    highest = jnp.maximum(
        jnp.max(old, axis=2, keepdims=True), jnp.max(new, axis=2, keepdims=True)
    )
    old = jnp.exp(old - highest)
    new = jnp.exp(new - highest)
    total = jnp.sum(old, axis=2, keepdims=True) + jnp.sum(new, axis=2, keepdims=True)
    inverse = 1.0 / total
    old_weight_ref[...] = (old * inverse).astype(jnp.bfloat16)
    new_weight_ref[...] = (new * inverse).astype(jnp.bfloat16)
    for job, (shift, g, group) in enumerate(jobs):
        attended = None
        for r in range(rows_local):
            term = jnp.dot(
                old_weight_ref[job], cache_ref[r, 1, group], preferred_element_type=jnp.float32
            )
            attended = term if attended is None else jnp.where(row_out == r, term, attended)
        value_new = pieces[shift][g, query_rows + pad :, :]
        attended = attended + jnp.dot(
            new_weight_ref[job], value_new, preferred_element_type=jnp.float32
        )
        outs[shift][g] = attended.astype(jnp.bfloat16)


def attend(pieces, cache, lengths, index, query_rows):
    groups, piece_rows, head_dim = pieces[0].shape
    slots, pad = cache.shape[3], (piece_rows - query_rows) // 2
    return pl.pallas_call(
        functools.partial(attend_kernel, len(pieces), query_rows),
        in_specs=[SMEM, SMEM] + [VMEM] * (1 + len(pieces)),
        out_specs=[VMEM] * len(pieces),
        out_shape=[jax.ShapeDtypeStruct((groups, query_rows, head_dim), jnp.bfloat16)]
        * len(pieces),
        scratch_shapes=[
            pltpu.VMEM((len(pieces) * groups, query_rows, count), kind)
            for kind in (jnp.float32, jnp.bfloat16)
            for count in (slots, pad)
        ],
        compiler_params=pltpu.CompilerParams(vmem_limit_bytes=SMALL_LIMIT),
        name="attend",
    )(index, lengths, cache, *pieces)


def gather_kernel(token_size, index_ref, *rest):
    pieces, (out_ref, block_ref) = rest[:-2], rest[-2:]
    count = len(pieces)
    groups, query_rows, head_dim = pieces[0].shape
    heads = query_rows // token_size
    for shift in range(count):
        source = wrap(index_ref[1] + shift, count)
        for g in range(groups):
            wide = pieces[shift][g].astype(jnp.float32)
            for head in range(heads):
                lane = (g * heads + head) * head_dim
                block_ref[source, :, lane : lane + head_dim] = wide[
                    head * token_size : (head + 1) * token_size, :
                ]
    for lane in range(0, groups * heads * head_dim, head_dim):
        part = block_ref[:, :, lane : lane + head_dim].reshape(count * token_size, head_dim)
        out_ref[:, lane : lane + head_dim] = part.astype(jnp.bfloat16)


def gather(pieces, index, token_size):
    groups, query_rows, head_dim = pieces[0].shape
    width = groups * (query_rows // token_size) * head_dim
    return pl.pallas_call(
        functools.partial(gather_kernel, token_size),
        in_specs=[SMEM] + [VMEM] * len(pieces),
        out_specs=VMEM,
        out_shape=jax.ShapeDtypeStruct((len(pieces) * token_size, width), jnp.bfloat16),
        scratch_shapes=[pltpu.VMEM((len(pieces), token_size, width), jnp.float32)],
        compiler_params=pltpu.CompilerParams(vmem_limit_bytes=SMALL_LIMIT),
        name="gather",
    )(index, *pieces)


def hold_kernel(first, after_ref, through_ref, source_ref, held_ref, same_ref, arrived):
    rows = pl.ds(first, held_ref.shape[0])
    copy = pltpu.make_async_copy(source_ref.at[rows], held_ref, arrived)
    copy.start()
    copy.wait()


def hold(source, first, count, after, through):
    return pl.pallas_call(
        functools.partial(hold_kernel, first),
        in_specs=[pl.BlockSpec(memory_space=space) for space in (pl.ANY, pl.ANY, pltpu.HBM)],
        out_specs=[VMEM, pl.BlockSpec(memory_space=pl.ANY)],
        out_shape=[
            pltpu.VMEM((count, source.shape[1]), source.dtype),
            jax.ShapeDtypeStruct(through.shape, through.dtype),
        ],
        input_output_aliases={1: 1},
        scratch_shapes=[pltpu.SemaphoreType.DMA],
        compiler_params=pltpu.CompilerParams(vmem_limit_bytes=2**20),
        cost_estimate=pl.CostEstimate(
            flops=0, bytes_accessed=count * source.shape[1] * 2, transcendentals=0
        ),
        name="hold",
    )(after, through, in_hbm(source))


def outward_kernel(block_count, axis_size, begin, held_count, index_ref, weight_ref, *rest):
    held, rest = rest[:held_count], rest[held_count:]
    blocks, rest = rest[:block_count], rest[block_count:]
    outs, (left_ref, total_ref, buffer, arrived) = rest[:axis_size], rest[axis_size:]
    token_count, depth = left_ref.shape
    size = token_count // block_count
    steps, step, width = buffer.shape
    kept = sum(part.shape[0] for part in held)

    copies = [
        pltpu.make_async_copy(
            weight_ref.at[pl.ds(kept + k * step, step), pl.ds(begin, width)],
            buffer.at[k],
            arrived.at[k],
        )
        for k in range(steps)
    ]
    for copy in copies:
        copy.start()
    for shift in range(block_count):
        source = wrap(index_ref[0] + block_count - shift, block_count)
        left_ref[pl.ds(pl.multiple_of(source * size, size), size), :] = blocks[shift][...]
    first = 0
    for part in held:
        term = jnp.dot(
            left_ref[:, first : first + part.shape[0]],
            part[:, begin : begin + width],
            preferred_element_type=jnp.float32,
        )
        if first == 0:
            total_ref[...] = term
        else:
            total_ref[...] += term
        first += part.shape[0]

    for k in range(steps):
        copies[k].wait()
        total_ref[...] += jnp.dot(
            left_ref[:, first + k * step : first + (k + 1) * step],
            buffer[k],
            preferred_element_type=jnp.float32,
        )
    rows = token_count // axis_size
    for shift in range(axis_size):
        first = pl.multiple_of(wrap(index_ref[1] + shift, axis_size) * rows, rows)
        outs[shift][...] = total_ref[pl.ds(first, rows), :].astype(outs[shift].dtype)


def outward(blocks, weight, held, begin, width, axis_size, index):
    size, depth = blocks[0].shape
    token_count = size * len(blocks)
    rows = token_count // axis_size
    streamed = depth - sum(part.shape[0] for part in held)
    steps = -(-streamed // OUTWARD_STEP)
    step = streamed // steps
    return pl.pallas_call(
        functools.partial(outward_kernel, len(blocks), axis_size, begin, len(held)),
        in_specs=[SMEM, pl.BlockSpec(memory_space=pltpu.HBM)] + [VMEM] * (len(held) + len(blocks)),
        out_specs=[VMEM] * axis_size,
        scratch_shapes=[
            pltpu.VMEM((token_count, depth), jnp.bfloat16),
            pltpu.VMEM((token_count, width), jnp.float32),
            pltpu.VMEM((steps, step, width), weight.dtype),
            pltpu.SemaphoreType.DMA((steps,)),
        ],
        out_shape=[
            jax.ShapeDtypeStruct((rows, width), jnp.bfloat16 if s else jnp.float32)
            for s in range(axis_size)
        ],
        compiler_params=pltpu.CompilerParams(vmem_limit_bytes=OUTWARD_LIMIT),
        cost_estimate=pl.CostEstimate(
            flops=2 * depth * width * token_count,
            bytes_accessed=2 * depth * width,
            transcendentals=0,
        ),
        name="outward",
    )(
        index,
        in_hbm(weight),
        *[pltpu.with_memory_space_constraint(part, pltpu.VMEM) for part in held],
        *blocks,
    )


def close_kernel(count, index_ref, tokens_ref, *rest):
    parts, out_ref = rest[:-1], rest[-1]
    rows, tokens, _ = out_ref.shape
    lanes = 128
    begin = 0
    for span in range(0, len(parts), count):
        width = parts[span].shape[1]
        for lane in range(0, width, lanes):
            total = parts[span][:, lane : lane + lanes]
            for part in parts[span + 1 : span + count]:
                total = total + part[:, lane : lane + lanes].astype(jnp.float32)
            at = begin + lane
            residual = tokens_ref[:, :, at : at + lanes].astype(jnp.float32)
            out_ref[:, :, at : at + lanes] = residual + total.reshape(rows, tokens, lanes)
        begin += width


def close(tokens, parts, head_devices, index):
    rows = tokens.shape[0] // head_devices
    shape = (rows,) + tokens.shape[1:]
    return pl.pallas_call(
        functools.partial(close_kernel, head_devices),
        grid_spec=pltpu.PrefetchScalarGridSpec(
            num_scalar_prefetch=1,
            grid=(1,),
            in_specs=[pl.BlockSpec(shape, lambda i, index: (index[1], 0, 0))]
            + [pl.BlockSpec(part.shape, lambda i, index: (0, 0)) for part in parts],
            out_specs=pl.BlockSpec(shape, lambda i, index: (0, 0, 0)),
        ),
        out_shape=jax.ShapeDtypeStruct(shape, jnp.float32),
        compiler_params=pltpu.CompilerParams(vmem_limit_bytes=SMALL_LIMIT),
        name="close",
    )(index, tokens, *parts)


def exchange(pieces, axis, sign=1):
    count = len(pieces)
    return [pieces[0]] + [
        lax.ppermute(pieces[s], axis, shift_pairs(count, sign * s)) for s in range(1, count)
    ]


def body(tokens, norm_gain, qkv_weight, out_weight, kv_cache, lengths, positions):
    rows_local = kv_cache.shape[0]
    width_devices = lax.axis_size("gx")
    head_devices = lax.axis_size("gy")
    index = jnp.stack([lax.axis_index("gx"), lax.axis_index("gy")])
    local_width = tokens.shape[2]
    head_dim = qkv_weight.shape[3]
    group_size = qkv_weight.shape[2] - 2
    token_size = rows_local * 2

    half = head_dim // 2
    frequency = rope_base ** (-2.0 * jnp.arange(half, dtype=jnp.float32) / head_dim)
    places = (positions[:, None] + jnp.arange(2, dtype=jnp.int32)[None, :]).astype(jnp.float32)
    angles = places.reshape(-1, 1) * frequency
    cosine = jnp.cos(angles)
    sine = jnp.sin(angles)
    cosine = jnp.concatenate([cosine, cosine], axis=1)
    sine = jnp.concatenate([-sine, sine], axis=1)
    cache = jnp.transpose(kv_cache, (0, 2, 3, 1, 4))

    parts = list(project(tokens, norm_gain, qkv_weight, width_devices, index))
    out_flat = out_weight.reshape(-1, local_width)
    cuts = [0]
    for share in HELD_SHARES:
        cuts.append(cuts[-1] + out_flat.shape[0] * share // 16)
    sizes = [end - begin for begin, end in zip(cuts, cuts[1:])]
    held = []

    def hold_beside(window, after, through):
        part, through = hold(out_flat, cuts[window], sizes[window], after, through)
        held.append(part)
        return through

    parts[0] = hold_beside(0, parts[1], parts[0])
    parts = exchange(parts, "gx")
    pieces = list(
        finish(parts, cosine, sine, cache, index, head_devices, token_size, head_dim)
    )
    pieces[0] = hold_beside(1, pieces[1], pieces[0])
    pieces = exchange(pieces, "gy")
    attended = list(attend(pieces, cache, lengths, index, group_size * token_size))
    attended[0] = hold_beside(2, attended[1], attended[0])
    attended = exchange(attended, "gy", -1)
    block = gather(attended, index, token_size)
    late = hold_beside(3, block, index + 0)
    blocks = exchange([block] * width_devices, "gx")
    cut = local_width * OUTWARD_SHARE // 16 // 128 * 128
    sums = []
    for begin, end in ((0, cut), (cut, local_width)):
        part = outward(blocks, out_flat, held, begin, end - begin, head_devices, late)
        sums += exchange(part, "gy")
    return close(tokens, sums, head_devices, index)


def solution(mesh):
    return jax.shard_map(
        body,
        mesh=mesh,
        in_specs=(
            P("groups", None, "gx"),
            P("gx"),
            P("gx", "gy", None, None),
            P("gy", None, "gx"),
            P(("groups", "gx", "gy"), None, None, None, None),
            P(("groups", "gx", "gy")),
            P("groups"),
        ),
        out_specs=P(("groups", "gy"), None, "gx"),
        check_vma=False,
    )
```

```python
import functools
import math

import jax
import jax.numpy as jnp
from jax import lax
from jax.experimental import pallas as pl
from jax.experimental.pallas import tpu as pltpu
from jax.sharding import PartitionSpec as P

D = 16384


norm_eps = 1e-05
rope_base = 500000.0
PROJECT_BLOCK = 512
PROJECT_SLOTS = 3
SMALL_LIMIT = 12 * 2**20
OUTWARD_SHARE = 8
OUTWARD_STEP = 1024
OUTWARD_LIMIT = 12 * 2**20
HELD_SHARES = (2, 4, 2, 7)
PAIR_GROUP = 4


def shift_pairs(count, shift):
    return [(i, (i + shift) % count) for i in range(count)]


def in_hbm(array):
    return pltpu.with_memory_space_constraint(array, pltpu.HBM)


def split_squares(total, lanes):
    high = total.astype(jnp.bfloat16).astype(jnp.float32)
    middle = (total - high).astype(jnp.bfloat16).astype(jnp.float32)
    low = total - high - middle
    lane = lax.broadcasted_iota(jnp.int32, (total.shape[0], lanes), 1)
    return jnp.where(
        lane == 0, high, jnp.where(lane == 1, middle, jnp.where(lane == 2, low, 0.0))
    )


def project_kernel(axis_size, block, slots, index_ref, tokens_hbm, gain_hbm, weight_ref, *rest):
    outs, rest = rest[:axis_size], rest[axis_size:]
    (
        hidden_ref,
        spread_ref,
        total_ref,
        sum_ref,
        gain_wide,
        tokens_ref,
        gain_ref,
        buffer,
        arrived,
    ) = rest
    total_rows, pair_rows, features = tokens_ref.shape
    token_count = total_rows * pair_rows
    pairs, mix, head_dim = weight_ref.shape[1:]
    groups = mix // 2
    steps = features // block
    lanes = 128

    def fetch(step, slot):
        return pltpu.make_async_copy(
            weight_ref.at[pl.ds(step * block, block)], buffer.at[slot], arrived.at[slot]
        )

    early = [
        pltpu.make_async_copy(tokens_hbm, tokens_ref, arrived.at[slots]),
        pltpu.make_async_copy(gain_hbm, gain_ref, arrived.at[slots + 1]),
    ]
    for copy in early:
        copy.start()
    for step in range(min(slots, steps)):
        fetch(step, step).start()

    wide = lanes * mix
    place = lax.broadcasted_iota(jnp.int32, (lanes, wide), 0)
    column = lax.broadcasted_iota(jnp.int32, (lanes, wide), 1)
    repeat = (column // mix == place).astype(jnp.bfloat16)
    member_of = lax.rem(lax.broadcasted_iota(jnp.int32, (token_count, wide), 1), mix)
    members = [(member_of == m).astype(jnp.bfloat16) for m in range(mix)]
    for copy in early:
        copy.wait()
    gain_wide[...] = gain_ref[...].astype(jnp.float32)
    squares = jnp.zeros((token_count, lanes), jnp.float32)
    group = 4
    for i in range(0, features // lanes, group):
        for j in range(group):
            at = (i + j) * lanes
            piece = tokens_ref[:, :, at : at + lanes].reshape(token_count, lanes)
            piece = piece.astype(jnp.float32)
            squares = squares + piece * piece
            hidden_ref[j * token_count : (j + 1) * token_count, :] = (
                piece * gain_wide[i + j : i + j + 1, :]
            ).astype(jnp.bfloat16)
        repeated = jnp.dot(hidden_ref[...], repeat, preferred_element_type=jnp.float32)
        repeated = repeated.astype(jnp.bfloat16)
        for j in range(group):
            for m in range(mix):
                spread_ref[
                    m * token_count : (m + 1) * token_count, (i + j) * wide : (i + j + 1) * wide
                ] = repeated[j * token_count : (j + 1) * token_count, :] * members[m]
    total_ref[...] = jnp.zeros_like(total_ref)

    @pl.loop(0, steps)
    def _(step):
        slot = lax.rem(step, slots)
        fetch(step, slot).wait()
        left = spread_ref.at[:, pl.ds(pl.multiple_of(step * block * mix, 128), block * mix)]
        for first in range(0, pairs, PAIR_GROUP):
            count = min(PAIR_GROUP, pairs - first)
            weights = [
                buffer[slot, :, first + i].reshape(block * mix, head_dim) for i in range(count)
            ]
            weights = jnp.concatenate(weights, axis=1) if count > 1 else weights[0]
            total_ref[:, first * head_dim : (first + count) * head_dim] += jnp.dot(
                left[...], weights, preferred_element_type=jnp.float32
            )

        @pl.when(step + slots < steps)
        def _():
            fetch(step + slots, slot).start()

    rows = token_count // axis_size
    sum_ref[...] = split_squares(jnp.sum(squares, axis=1, keepdims=True), lanes)
    for shift in range(axis_size):
        owner = lax.rem(index_ref[0] + shift, axis_size)
        first = pl.multiple_of(owner * rows, rows)
        own = outs[shift]
        for g in range(groups):
            for head in range(2 * pairs):
                start = ((head % 2) * groups + g) * token_count
                lane = (head // 2) * head_dim
                own[g, :, head * head_dim : (head + 1) * head_dim] = total_ref[
                    pl.ds(start + first, rows), lane : lane + head_dim
                ].astype(own.dtype)
            own[g, :, 2 * pairs * head_dim :] = sum_ref[pl.ds(first, rows), :].astype(own.dtype)


def project(tokens, norm_gain, qkv_weight, axis_size, index):
    features, groups, heads, head_dim = qkv_weight.shape
    token_count = tokens.shape[0] * tokens.shape[1]
    mix = 2 * groups
    pairs = heads // 2
    block = min(features, PROJECT_BLOCK)
    slots = PROJECT_SLOTS
    rows = token_count // axis_size
    width = heads * head_dim + 128
    weight = jnp.transpose(qkv_weight, (0, 2, 1, 3)).reshape(features, pairs, mix, head_dim)
    return pl.pallas_call(
        functools.partial(project_kernel, axis_size, block, slots),
        in_specs=[
            pl.BlockSpec(memory_space=pltpu.SMEM),
            pl.BlockSpec(memory_space=pltpu.HBM),
            pl.BlockSpec(memory_space=pltpu.HBM),
            pl.BlockSpec(memory_space=pltpu.HBM),
        ],
        out_specs=[pl.BlockSpec(memory_space=pltpu.VMEM)] * axis_size,
        scratch_shapes=[
            pltpu.VMEM((4 * token_count, 128), jnp.bfloat16),
            pltpu.VMEM((mix * token_count, features * mix), jnp.bfloat16),
            pltpu.VMEM((mix * token_count, pairs * head_dim), jnp.float32),
            pltpu.VMEM((token_count, 128), jnp.float32),
            pltpu.VMEM((features // 128, 128), jnp.float32),
            pltpu.VMEM(tokens.shape, tokens.dtype),
            pltpu.VMEM((features // 128, 128), norm_gain.dtype),
            pltpu.VMEM((slots, block, pairs, mix, head_dim), jnp.bfloat16),
            pltpu.SemaphoreType.DMA((slots + 2,)),
        ],
        out_shape=[
            jax.ShapeDtypeStruct((groups, rows, width), jnp.bfloat16 if s else jnp.float32)
            for s in range(axis_size)
        ],
        compiler_params=pltpu.CompilerParams(vmem_limit_bytes=48 * 2**20),
        cost_estimate=pl.CostEstimate(
            flops=2 * qkv_weight.size * token_count,
            bytes_accessed=qkv_weight.size * 2,
            transcendentals=0,
        ),
        name="project",
    )(index, *[in_hbm(array) for array in (tokens, norm_gain.reshape(-1, 128), weight)])


SMEM = pl.BlockSpec(memory_space=pltpu.SMEM)
VMEM = pl.BlockSpec(memory_space=pltpu.VMEM)


def wrap(place, count):
    return lax.rem(place, count)


def finish_kernel(
    width_devices, head_devices, token_size, head_dim, index_ref, _, cosine_ref, sine_ref, *rest
):
    parts, rest = rest[:width_devices], rest[width_devices:]
    outs, (turned_ref, piece_ref) = rest[:head_devices], rest[head_devices:]
    groups, rows, width = parts[0].shape
    heads = width // head_dim - 1
    group_size = heads - 2
    pad = (piece_ref.shape[0] - group_size * token_size) // 2

    def added(g, lane):
        total = parts[0][g, :, lane : lane + head_dim]
        for part in parts[1:]:
            total = total + part[g, :, lane : lane + head_dim].astype(jnp.float32)
        return total

    squares = jnp.sum(added(0, heads * head_dim), axis=1, keepdims=True)
    inv_rms = lax.rsqrt(squares / D + norm_eps)
    start = pl.multiple_of(index_ref[0] * rows, rows)
    cosine = cosine_ref[pl.ds(start, rows), :]
    sine = sine_ref[pl.ds(start, rows), :]
    for g in range(groups):
        for head in range(heads):
            value = added(g, head * head_dim) * inv_rms
            if head <= group_size:
                value = value * cosine + pltpu.roll(value, head_dim // 2, 1) * sine
            turned_ref[g, head] = value.reshape(head_devices, token_size, head_dim)
    piece_ref[...] = jnp.zeros_like(piece_ref)
    for shift in range(head_devices):
        owner = wrap(index_ref[1] + shift, head_devices)
        for g in range(groups):
            for head in range(heads):
                at = head * token_size
                if head >= group_size:
                    at = group_size * token_size + (head - group_size) * pad
                piece_ref[at : at + token_size, :] = turned_ref[g, head, owner]
            outs[shift][g] = piece_ref[...].astype(jnp.bfloat16)


def finish(parts, cosine, sine, early, index, head_devices, token_size, head_dim):
    groups, rows, width = parts[0].shape
    heads = width // head_dim - 1
    piece_rows = (heads - 2) * token_size + 2 * (-(-token_size // 16) * 16)
    return pl.pallas_call(
        functools.partial(finish_kernel, len(parts), head_devices, token_size, head_dim),
        in_specs=[SMEM, pl.BlockSpec(memory_space=pl.ANY)] + [VMEM] * (2 + len(parts)),
        out_specs=[VMEM] * head_devices,
        out_shape=[jax.ShapeDtypeStruct((groups, piece_rows, head_dim), jnp.bfloat16)]
        * head_devices,
        scratch_shapes=[
            pltpu.VMEM((groups, heads, head_devices, token_size, head_dim), jnp.float32),
            pltpu.VMEM((piece_rows, head_dim), jnp.float32),
        ],
        compiler_params=pltpu.CompilerParams(vmem_limit_bytes=SMALL_LIMIT),
        name="finish",
    )(index, early, cosine, sine, *parts)


def attend_kernel(head_devices, query_rows, index_ref, length_ref, cache_ref, *rest):
    pieces, rest = rest[:head_devices], rest[head_devices:]
    outs, rest = rest[:head_devices], rest[head_devices:]
    old_ref, new_ref, old_weight_ref, new_weight_ref = rest
    groups, piece_rows, head_dim = pieces[0].shape
    rows_local, _, _, slots, _ = cache_ref.shape
    pad = (piece_rows - query_rows) // 2
    token_size = 2 * rows_local
    scale = 1.0 / math.sqrt(head_dim)
    token_old = lax.rem(lax.broadcasted_iota(jnp.int32, (query_rows, slots), 0), token_size)
    slot = lax.broadcasted_iota(jnp.int32, (query_rows, slots), 1)
    length = jnp.zeros((query_rows, slots), jnp.int32)
    for r in range(rows_local):
        length = jnp.where(token_old // 2 == r, length_ref[r], length)
    visible = slot < length
    token = lax.rem(lax.broadcasted_iota(jnp.int32, (query_rows, pad), 0), token_size)
    other = lax.broadcasted_iota(jnp.int32, (query_rows, pad), 1)
    causal = (other // 2 == token // 2) & (other <= token)
    row_out = lax.rem(lax.broadcasted_iota(jnp.int32, (query_rows, head_dim), 0), token_size) // 2
    last = (((1,), (1,)), ((), ()))
    jobs = []
    for shift in range(head_devices):
        source = wrap(index_ref[1] + head_devices - shift, head_devices)
        jobs += [(shift, g, source * groups + g) for g in range(groups)]
    for job, (shift, g, group) in enumerate(jobs):
        queries = pieces[shift][g, :query_rows, :]
        old = None
        for r in range(rows_local):
            term = lax.dot_general(
                queries, cache_ref[r, 0, group], last, preferred_element_type=jnp.float32
            )
            old = term if old is None else jnp.where(token_old // 2 == r, term, old)
        old_ref[job] = jnp.where(visible, old * scale, -1e30)
        key_new = pieces[shift][g, query_rows : query_rows + pad, :]
        new = lax.dot_general(queries, key_new, last, preferred_element_type=jnp.float32)
        new_ref[job] = jnp.where(causal, new * scale, -1e30)
    old = old_ref[...]
    new = new_ref[...]
    highest = jnp.maximum(
        jnp.max(old, axis=2, keepdims=True), jnp.max(new, axis=2, keepdims=True)
    )
    old = jnp.exp(old - highest)
    new = jnp.exp(new - highest)
    total = jnp.sum(old, axis=2, keepdims=True) + jnp.sum(new, axis=2, keepdims=True)
    inverse = 1.0 / total
    old_weight_ref[...] = (old * inverse).astype(jnp.bfloat16)
    new_weight_ref[...] = (new * inverse).astype(jnp.bfloat16)
    for job, (shift, g, group) in enumerate(jobs):
        attended = None
        for r in range(rows_local):
            term = jnp.dot(
                old_weight_ref[job], cache_ref[r, 1, group], preferred_element_type=jnp.float32
            )
            attended = term if attended is None else jnp.where(row_out == r, term, attended)
        value_new = pieces[shift][g, query_rows + pad :, :]
        attended = attended + jnp.dot(
            new_weight_ref[job], value_new, preferred_element_type=jnp.float32
        )
        outs[shift][g] = attended.astype(jnp.bfloat16)


def attend(pieces, cache, lengths, index, query_rows):
    groups, piece_rows, head_dim = pieces[0].shape
    slots, pad = cache.shape[3], (piece_rows - query_rows) // 2
    return pl.pallas_call(
        functools.partial(attend_kernel, len(pieces), query_rows),
        in_specs=[SMEM, SMEM] + [VMEM] * (1 + len(pieces)),
        out_specs=[VMEM] * len(pieces),
        out_shape=[jax.ShapeDtypeStruct((groups, query_rows, head_dim), jnp.bfloat16)]
        * len(pieces),
        scratch_shapes=[
            pltpu.VMEM((len(pieces) * groups, query_rows, count), kind)
            for kind in (jnp.float32, jnp.bfloat16)
            for count in (slots, pad)
        ],
        compiler_params=pltpu.CompilerParams(vmem_limit_bytes=SMALL_LIMIT),
        name="attend",
    )(index, lengths, cache, *pieces)


def gather_kernel(token_size, index_ref, *rest):
    pieces, (out_ref, block_ref) = rest[:-2], rest[-2:]
    count = len(pieces)
    groups, query_rows, head_dim = pieces[0].shape
    heads = query_rows // token_size
    for shift in range(count):
        source = wrap(index_ref[1] + shift, count)
        for g in range(groups):
            wide = pieces[shift][g].astype(jnp.float32)
            for head in range(heads):
                lane = (g * heads + head) * head_dim
                block_ref[source, :, lane : lane + head_dim] = wide[
                    head * token_size : (head + 1) * token_size, :
                ]
    for lane in range(0, groups * heads * head_dim, head_dim):
        part = block_ref[:, :, lane : lane + head_dim].reshape(count * token_size, head_dim)
        out_ref[:, lane : lane + head_dim] = part.astype(jnp.bfloat16)


def gather(pieces, index, token_size):
    groups, query_rows, head_dim = pieces[0].shape
    width = groups * (query_rows // token_size) * head_dim
    return pl.pallas_call(
        functools.partial(gather_kernel, token_size),
        in_specs=[SMEM] + [VMEM] * len(pieces),
        out_specs=VMEM,
        out_shape=jax.ShapeDtypeStruct((len(pieces) * token_size, width), jnp.bfloat16),
        scratch_shapes=[pltpu.VMEM((len(pieces), token_size, width), jnp.float32)],
        compiler_params=pltpu.CompilerParams(vmem_limit_bytes=SMALL_LIMIT),
        name="gather",
    )(index, *pieces)


def hold_kernel(first, after_ref, through_ref, source_ref, held_ref, same_ref, arrived):
    rows = pl.ds(first, held_ref.shape[0])
    copy = pltpu.make_async_copy(source_ref.at[rows], held_ref, arrived)
    copy.start()
    copy.wait()


def hold(source, first, count, after, through):
    return pl.pallas_call(
        functools.partial(hold_kernel, first),
        in_specs=[pl.BlockSpec(memory_space=space) for space in (pl.ANY, pl.ANY, pltpu.HBM)],
        out_specs=[VMEM, pl.BlockSpec(memory_space=pl.ANY)],
        out_shape=[
            pltpu.VMEM((count, source.shape[1]), source.dtype),
            jax.ShapeDtypeStruct(through.shape, through.dtype),
        ],
        input_output_aliases={1: 1},
        scratch_shapes=[pltpu.SemaphoreType.DMA],
        compiler_params=pltpu.CompilerParams(vmem_limit_bytes=2**20),
        cost_estimate=pl.CostEstimate(
            flops=0, bytes_accessed=count * source.shape[1] * 2, transcendentals=0
        ),
        name="hold",
    )(after, through, in_hbm(source))


def outward_kernel(block_count, axis_size, begin, held_count, index_ref, weight_ref, *rest):
    held, rest = rest[:held_count], rest[held_count:]
    blocks, rest = rest[:block_count], rest[block_count:]
    outs, (left_ref, total_ref, buffer, arrived) = rest[:axis_size], rest[axis_size:]
    token_count, depth = left_ref.shape
    size = token_count // block_count
    steps, step, width = buffer.shape
    kept = sum(part.shape[0] for part in held)

    copies = [
        pltpu.make_async_copy(
            weight_ref.at[pl.ds(kept + k * step, step), pl.ds(begin, width)],
            buffer.at[k],
            arrived.at[k],
        )
        for k in range(steps)
    ]
    for copy in copies:
        copy.start()
    for shift in range(block_count):
        source = wrap(index_ref[0] + block_count - shift, block_count)
        left_ref[pl.ds(pl.multiple_of(source * size, size), size), :] = blocks[shift][...]
    first = 0
    for part in held:
        term = jnp.dot(
            left_ref[:, first : first + part.shape[0]],
            part[:, begin : begin + width],
            preferred_element_type=jnp.float32,
        )
        if first == 0:
            total_ref[...] = term
        else:
            total_ref[...] += term
        first += part.shape[0]

    for k in range(steps):
        copies[k].wait()
        total_ref[...] += jnp.dot(
            left_ref[:, first + k * step : first + (k + 1) * step],
            buffer[k],
            preferred_element_type=jnp.float32,
        )
    rows = token_count // axis_size
    for shift in range(axis_size):
        first = pl.multiple_of(wrap(index_ref[1] + axis_size - shift, axis_size) * rows, rows)
        outs[shift][...] = total_ref[pl.ds(first, rows), :].astype(outs[shift].dtype)


def outward(blocks, weight, held, begin, width, axis_size, index):
    size, depth = blocks[0].shape
    token_count = size * len(blocks)
    rows = token_count // axis_size
    streamed = depth - sum(part.shape[0] for part in held)
    steps = -(-streamed // OUTWARD_STEP)
    step = streamed // steps
    return pl.pallas_call(
        functools.partial(outward_kernel, len(blocks), axis_size, begin, len(held)),
        in_specs=[SMEM, pl.BlockSpec(memory_space=pltpu.HBM)] + [VMEM] * (len(held) + len(blocks)),
        out_specs=[VMEM] * axis_size,
        scratch_shapes=[
            pltpu.VMEM((token_count, depth), jnp.bfloat16),
            pltpu.VMEM((token_count, width), jnp.float32),
            pltpu.VMEM((steps, step, width), weight.dtype),
            pltpu.SemaphoreType.DMA((steps,)),
        ],
        out_shape=[
            jax.ShapeDtypeStruct((rows, width), jnp.bfloat16 if s else jnp.float32)
            for s in range(axis_size)
        ],
        compiler_params=pltpu.CompilerParams(vmem_limit_bytes=OUTWARD_LIMIT),
        cost_estimate=pl.CostEstimate(
            flops=2 * depth * width * token_count,
            bytes_accessed=2 * depth * width,
            transcendentals=0,
        ),
        name="outward",
    )(
        index,
        in_hbm(weight),
        *[pltpu.with_memory_space_constraint(part, pltpu.VMEM) for part in held],
        *blocks,
    )


def close_kernel(count, index_ref, tokens_ref, *rest):
    parts, out_ref = rest[:-1], rest[-1]
    rows, tokens, _ = out_ref.shape
    lanes = 128
    begin = 0
    for span in range(0, len(parts), count):
        width = parts[span].shape[1]
        for lane in range(0, width, lanes):
            total = parts[span][:, lane : lane + lanes]
            for part in parts[span + 1 : span + count]:
                total = total + part[:, lane : lane + lanes].astype(jnp.float32)
            at = begin + lane
            residual = tokens_ref[:, :, at : at + lanes].astype(jnp.float32)
            out_ref[:, :, at : at + lanes] = residual + total.reshape(rows, tokens, lanes)
        begin += width


def close(tokens, parts, head_devices, index):
    rows = tokens.shape[0] // head_devices
    shape = (rows,) + tokens.shape[1:]
    return pl.pallas_call(
        functools.partial(close_kernel, head_devices),
        grid_spec=pltpu.PrefetchScalarGridSpec(
            num_scalar_prefetch=1,
            grid=(1,),
            in_specs=[pl.BlockSpec(shape, lambda i, index: (index[1], 0, 0))]
            + [pl.BlockSpec(part.shape, lambda i, index: (0, 0)) for part in parts],
            out_specs=pl.BlockSpec(shape, lambda i, index: (0, 0, 0)),
        ),
        out_shape=jax.ShapeDtypeStruct(shape, jnp.float32),
        compiler_params=pltpu.CompilerParams(vmem_limit_bytes=SMALL_LIMIT),
        name="close",
    )(index, tokens, *parts)


def exchange(pieces, axis, sign=1):
    count = len(pieces)
    return [pieces[0]] + [
        lax.ppermute(pieces[s], axis, shift_pairs(count, sign * s)) for s in range(1, count)
    ]


def body(tokens, norm_gain, qkv_weight, out_weight, kv_cache, lengths, positions):
    rows_local = kv_cache.shape[0]
    width_devices = lax.axis_size("gx")
    head_devices = lax.axis_size("gy")
    index = jnp.stack([lax.axis_index("gx"), lax.axis_index("gy")])
    local_width = tokens.shape[2]
    head_dim = qkv_weight.shape[3]
    group_size = qkv_weight.shape[2] - 2
    token_size = rows_local * 2

    half = head_dim // 2
    frequency = rope_base ** (-2.0 * jnp.arange(half, dtype=jnp.float32) / head_dim)
    places = (positions[:, None] + jnp.arange(2, dtype=jnp.int32)[None, :]).astype(jnp.float32)
    angles = places.reshape(-1, 1) * frequency
    cosine = jnp.cos(angles)
    sine = jnp.sin(angles)
    cosine = jnp.concatenate([cosine, cosine], axis=1)
    sine = jnp.concatenate([-sine, sine], axis=1)
    cache = jnp.transpose(kv_cache, (0, 2, 3, 1, 4))

    parts = list(project(tokens, norm_gain, qkv_weight, width_devices, index))
    out_flat = out_weight.reshape(-1, local_width)
    cuts = [0]
    for share in HELD_SHARES:
        cuts.append(cuts[-1] + out_flat.shape[0] * share // 16)
    sizes = [end - begin for begin, end in zip(cuts, cuts[1:])]
    held = []

    def hold_beside(window, after, through):
        part, through = hold(out_flat, cuts[window], sizes[window], after, through)
        held.append(part)
        return through

    parts[0] = hold_beside(0, parts[1], parts[0])
    parts = exchange(parts, "gx")
    pieces = list(
        finish(parts, cosine, sine, cache, index, head_devices, token_size, head_dim)
    )
    pieces[0] = hold_beside(1, pieces[1], pieces[0])
    pieces = exchange(pieces, "gy")
    attended = list(attend(pieces, cache, lengths, index, group_size * token_size))
    attended[0] = hold_beside(2, attended[1], attended[0])
    attended = exchange(attended, "gy", -1)
    block = gather(attended, index, token_size)
    late = hold_beside(3, block, index + 0)
    blocks = exchange([block] * width_devices, "gx")
    cut = local_width * OUTWARD_SHARE // 16 // 128 * 128
    sums = []
    for begin, end in ((0, cut), (cut, local_width)):
        part = outward(blocks, out_flat, held, begin, end - begin, head_devices, late)
        sums += exchange(part, "gy", -1)
    return close(tokens, sums, head_devices, index)


def solution(mesh):
    return jax.shard_map(
        body,
        mesh=mesh,
        in_specs=(
            P("groups", None, "gx"),
            P("gx"),
            P("gx", "gy", None, None),
            P("gy", None, "gx"),
            P(("groups", "gx", "gy"), None, None, None, None),
            P(("groups", "gx", "gy")),
            P("groups"),
        ),
        out_specs=P(("groups", "gy"), None, "gx"),
        check_vma=False,
    )
```

```python
import functools
import math

import jax
import jax.numpy as jnp
from jax import lax
from jax.experimental import pallas as pl
from jax.experimental.pallas import tpu as pltpu
from jax.sharding import PartitionSpec as P

D = 16384


norm_eps = 1e-05
rope_base = 500000.0
PROJECT_BLOCK = 512
PROJECT_SLOTS = 3
SMALL_LIMIT = 12 * 2**20
OUTWARD_SHARE = 8
OUTWARD_STEP = 1024
OUTWARD_LIMIT = 12 * 2**20
HELD_SHARES = (2, 3, 3, 7)
PAIR_GROUP = 4


def shift_pairs(count, shift):
    return [(i, (i + shift) % count) for i in range(count)]


def in_hbm(array):
    return pltpu.with_memory_space_constraint(array, pltpu.HBM)


def split_squares(total, lanes):
    high = total.astype(jnp.bfloat16).astype(jnp.float32)
    middle = (total - high).astype(jnp.bfloat16).astype(jnp.float32)
    low = total - high - middle
    lane = lax.broadcasted_iota(jnp.int32, (total.shape[0], lanes), 1)
    return jnp.where(
        lane == 0, high, jnp.where(lane == 1, middle, jnp.where(lane == 2, low, 0.0))
    )


def project_kernel(axis_size, block, slots, index_ref, tokens_hbm, gain_hbm, weight_ref, *rest):
    outs, rest = rest[:axis_size], rest[axis_size:]
    (
        hidden_ref,
        spread_ref,
        total_ref,
        sum_ref,
        gain_wide,
        tokens_ref,
        gain_ref,
        buffer,
        arrived,
    ) = rest
    total_rows, pair_rows, features = tokens_ref.shape
    token_count = total_rows * pair_rows
    pairs, mix, head_dim = weight_ref.shape[1:]
    groups = mix // 2
    steps = features // block
    lanes = 128

    def fetch(step, slot):
        return pltpu.make_async_copy(
            weight_ref.at[pl.ds(step * block, block)], buffer.at[slot], arrived.at[slot]
        )

    early = [
        pltpu.make_async_copy(tokens_hbm, tokens_ref, arrived.at[slots]),
        pltpu.make_async_copy(gain_hbm, gain_ref, arrived.at[slots + 1]),
    ]
    for copy in early:
        copy.start()
    for step in range(min(slots, steps)):
        fetch(step, step).start()

    wide = lanes * mix
    place = lax.broadcasted_iota(jnp.int32, (lanes, wide), 0)
    column = lax.broadcasted_iota(jnp.int32, (lanes, wide), 1)
    repeat = (column // mix == place).astype(jnp.bfloat16)
    member_of = lax.rem(lax.broadcasted_iota(jnp.int32, (token_count, wide), 1), mix)
    members = [(member_of == m).astype(jnp.bfloat16) for m in range(mix)]
    for copy in early:
        copy.wait()
    gain_wide[...] = gain_ref[...].astype(jnp.float32)
    squares = jnp.zeros((token_count, lanes), jnp.float32)
    group = 4
    for i in range(0, features // lanes, group):
        for j in range(group):
            at = (i + j) * lanes
            piece = tokens_ref[:, :, at : at + lanes].reshape(token_count, lanes)
            piece = piece.astype(jnp.float32)
            squares = squares + piece * piece
            hidden_ref[j * token_count : (j + 1) * token_count, :] = (
                piece * gain_wide[i + j : i + j + 1, :]
            ).astype(jnp.bfloat16)
        repeated = jnp.dot(hidden_ref[...], repeat, preferred_element_type=jnp.float32)
        repeated = repeated.astype(jnp.bfloat16)
        for j in range(group):
            for m in range(mix):
                spread_ref[
                    m * token_count : (m + 1) * token_count, (i + j) * wide : (i + j + 1) * wide
                ] = repeated[j * token_count : (j + 1) * token_count, :] * members[m]
    total_ref[...] = jnp.zeros_like(total_ref)

    @pl.loop(0, steps)
    def _(step):
        slot = lax.rem(step, slots)
        fetch(step, slot).wait()
        left = spread_ref.at[:, pl.ds(pl.multiple_of(step * block * mix, 128), block * mix)]
        for first in range(0, pairs, PAIR_GROUP):
            count = min(PAIR_GROUP, pairs - first)
            weights = [
                buffer[slot, :, first + i].reshape(block * mix, head_dim) for i in range(count)
            ]
            weights = jnp.concatenate(weights, axis=1) if count > 1 else weights[0]
            total_ref[:, first * head_dim : (first + count) * head_dim] += jnp.dot(
                left[...], weights, preferred_element_type=jnp.float32
            )

        @pl.when(step + slots < steps)
        def _():
            fetch(step + slots, slot).start()

    rows = token_count // axis_size
    sum_ref[...] = split_squares(jnp.sum(squares, axis=1, keepdims=True), lanes)
    for shift in range(axis_size):
        owner = lax.rem(index_ref[0] + shift, axis_size)
        first = pl.multiple_of(owner * rows, rows)
        own = outs[shift]
        for g in range(groups):
            for head in range(2 * pairs):
                start = ((head % 2) * groups + g) * token_count
                lane = (head // 2) * head_dim
                own[g, :, head * head_dim : (head + 1) * head_dim] = total_ref[
                    pl.ds(start + first, rows), lane : lane + head_dim
                ].astype(own.dtype)
            own[g, :, 2 * pairs * head_dim :] = sum_ref[pl.ds(first, rows), :].astype(own.dtype)


def project(tokens, norm_gain, qkv_weight, axis_size, index):
    features, groups, heads, head_dim = qkv_weight.shape
    token_count = tokens.shape[0] * tokens.shape[1]
    mix = 2 * groups
    pairs = heads // 2
    block = min(features, PROJECT_BLOCK)
    slots = PROJECT_SLOTS
    rows = token_count // axis_size
    width = heads * head_dim + 128
    weight = jnp.transpose(qkv_weight, (0, 2, 1, 3)).reshape(features, pairs, mix, head_dim)
    return pl.pallas_call(
        functools.partial(project_kernel, axis_size, block, slots),
        in_specs=[
            pl.BlockSpec(memory_space=pltpu.SMEM),
            pl.BlockSpec(memory_space=pltpu.HBM),
            pl.BlockSpec(memory_space=pltpu.HBM),
            pl.BlockSpec(memory_space=pltpu.HBM),
        ],
        out_specs=[pl.BlockSpec(memory_space=pltpu.VMEM)] * axis_size,
        scratch_shapes=[
            pltpu.VMEM((4 * token_count, 128), jnp.bfloat16),
            pltpu.VMEM((mix * token_count, features * mix), jnp.bfloat16),
            pltpu.VMEM((mix * token_count, pairs * head_dim), jnp.float32),
            pltpu.VMEM((token_count, 128), jnp.float32),
            pltpu.VMEM((features // 128, 128), jnp.float32),
            pltpu.VMEM(tokens.shape, tokens.dtype),
            pltpu.VMEM((features // 128, 128), norm_gain.dtype),
            pltpu.VMEM((slots, block, pairs, mix, head_dim), jnp.bfloat16),
            pltpu.SemaphoreType.DMA((slots + 2,)),
        ],
        out_shape=[
            jax.ShapeDtypeStruct((groups, rows, width), jnp.bfloat16 if s else jnp.float32)
            for s in range(axis_size)
        ],
        compiler_params=pltpu.CompilerParams(vmem_limit_bytes=48 * 2**20),
        cost_estimate=pl.CostEstimate(
            flops=2 * qkv_weight.size * token_count,
            bytes_accessed=qkv_weight.size * 2,
            transcendentals=0,
        ),
        name="project",
    )(index, *[in_hbm(array) for array in (tokens, norm_gain.reshape(-1, 128), weight)])


SMEM = pl.BlockSpec(memory_space=pltpu.SMEM)
VMEM = pl.BlockSpec(memory_space=pltpu.VMEM)


def wrap(place, count):
    return lax.rem(place, count)


def finish_kernel(
    width_devices, head_devices, token_size, head_dim, index_ref, _, cosine_ref, sine_ref, *rest
):
    parts, rest = rest[:width_devices], rest[width_devices:]
    outs, (turned_ref, piece_ref) = rest[:head_devices], rest[head_devices:]
    groups, rows, width = parts[0].shape
    heads = width // head_dim - 1
    group_size = heads - 2
    pad = (piece_ref.shape[0] - group_size * token_size) // 2

    def added(g, lane):
        total = parts[0][g, :, lane : lane + head_dim]
        for part in parts[1:]:
            total = total + part[g, :, lane : lane + head_dim].astype(jnp.float32)
        return total

    squares = jnp.sum(added(0, heads * head_dim), axis=1, keepdims=True)
    inv_rms = lax.rsqrt(squares / D + norm_eps)
    start = pl.multiple_of(index_ref[0] * rows, rows)
    cosine = cosine_ref[pl.ds(start, rows), :]
    sine = sine_ref[pl.ds(start, rows), :]
    for g in range(groups):
        for head in range(heads):
            value = added(g, head * head_dim) * inv_rms
            if head <= group_size:
                value = value * cosine + pltpu.roll(value, head_dim // 2, 1) * sine
            turned_ref[g, head] = value.reshape(head_devices, token_size, head_dim)
    piece_ref[...] = jnp.zeros_like(piece_ref)
    for shift in range(head_devices):
        owner = wrap(index_ref[1] + shift, head_devices)
        for g in range(groups):
            for head in range(heads):
                at = head * token_size
                if head >= group_size:
                    at = group_size * token_size + (head - group_size) * pad
                piece_ref[at : at + token_size, :] = turned_ref[g, head, owner]
            outs[shift][g] = piece_ref[...].astype(jnp.bfloat16)


def finish(parts, cosine, sine, early, index, head_devices, token_size, head_dim):
    groups, rows, width = parts[0].shape
    heads = width // head_dim - 1
    piece_rows = (heads - 2) * token_size + 2 * (-(-token_size // 16) * 16)
    return pl.pallas_call(
        functools.partial(finish_kernel, len(parts), head_devices, token_size, head_dim),
        in_specs=[SMEM, pl.BlockSpec(memory_space=pl.ANY)] + [VMEM] * (2 + len(parts)),
        out_specs=[VMEM] * head_devices,
        out_shape=[jax.ShapeDtypeStruct((groups, piece_rows, head_dim), jnp.bfloat16)]
        * head_devices,
        scratch_shapes=[
            pltpu.VMEM((groups, heads, head_devices, token_size, head_dim), jnp.float32),
            pltpu.VMEM((piece_rows, head_dim), jnp.float32),
        ],
        compiler_params=pltpu.CompilerParams(vmem_limit_bytes=SMALL_LIMIT),
        name="finish",
    )(index, early, cosine, sine, *parts)


def attend_kernel(head_devices, query_rows, index_ref, length_ref, cache_ref, *rest):
    pieces, rest = rest[:head_devices], rest[head_devices:]
    outs, rest = rest[:head_devices], rest[head_devices:]
    old_ref, new_ref, old_weight_ref, new_weight_ref = rest
    groups, piece_rows, head_dim = pieces[0].shape
    rows_local, _, _, slots, _ = cache_ref.shape
    pad = (piece_rows - query_rows) // 2
    token_size = 2 * rows_local
    scale = 1.0 / math.sqrt(head_dim)
    token_old = lax.rem(lax.broadcasted_iota(jnp.int32, (query_rows, slots), 0), token_size)
    slot = lax.broadcasted_iota(jnp.int32, (query_rows, slots), 1)
    length = jnp.zeros((query_rows, slots), jnp.int32)
    for r in range(rows_local):
        length = jnp.where(token_old // 2 == r, length_ref[r], length)
    visible = slot < length
    token = lax.rem(lax.broadcasted_iota(jnp.int32, (query_rows, pad), 0), token_size)
    other = lax.broadcasted_iota(jnp.int32, (query_rows, pad), 1)
    causal = (other // 2 == token // 2) & (other <= token)
    row_out = lax.rem(lax.broadcasted_iota(jnp.int32, (query_rows, head_dim), 0), token_size) // 2
    last = (((1,), (1,)), ((), ()))
    jobs = []
    for shift in range(head_devices):
        source = wrap(index_ref[1] + head_devices - shift, head_devices)
        jobs += [(shift, g, source * groups + g) for g in range(groups)]
    for job, (shift, g, group) in enumerate(jobs):
        queries = pieces[shift][g, :query_rows, :]
        old = None
        for r in range(rows_local):
            term = lax.dot_general(
                queries, cache_ref[r, 0, group], last, preferred_element_type=jnp.float32
            )
            old = term if old is None else jnp.where(token_old // 2 == r, term, old)
        old_ref[job] = jnp.where(visible, old * scale, -1e30)
        key_new = pieces[shift][g, query_rows : query_rows + pad, :]
        new = lax.dot_general(queries, key_new, last, preferred_element_type=jnp.float32)
        new_ref[job] = jnp.where(causal, new * scale, -1e30)
    old = old_ref[...]
    new = new_ref[...]
    highest = jnp.maximum(
        jnp.max(old, axis=2, keepdims=True), jnp.max(new, axis=2, keepdims=True)
    )
    old = jnp.exp(old - highest)
    new = jnp.exp(new - highest)
    total = jnp.sum(old, axis=2, keepdims=True) + jnp.sum(new, axis=2, keepdims=True)
    inverse = 1.0 / total
    old_weight_ref[...] = (old * inverse).astype(jnp.bfloat16)
    new_weight_ref[...] = (new * inverse).astype(jnp.bfloat16)
    for job, (shift, g, group) in enumerate(jobs):
        attended = None
        for r in range(rows_local):
            term = jnp.dot(
                old_weight_ref[job], cache_ref[r, 1, group], preferred_element_type=jnp.float32
            )
            attended = term if attended is None else jnp.where(row_out == r, term, attended)
        value_new = pieces[shift][g, query_rows + pad :, :]
        attended = attended + jnp.dot(
            new_weight_ref[job], value_new, preferred_element_type=jnp.float32
        )
        outs[shift][g] = attended.astype(jnp.bfloat16)


def attend(pieces, cache, lengths, index, query_rows):
    groups, piece_rows, head_dim = pieces[0].shape
    slots, pad = cache.shape[3], (piece_rows - query_rows) // 2
    return pl.pallas_call(
        functools.partial(attend_kernel, len(pieces), query_rows),
        in_specs=[SMEM, SMEM] + [VMEM] * (1 + len(pieces)),
        out_specs=[VMEM] * len(pieces),
        out_shape=[jax.ShapeDtypeStruct((groups, query_rows, head_dim), jnp.bfloat16)]
        * len(pieces),
        scratch_shapes=[
            pltpu.VMEM((len(pieces) * groups, query_rows, count), kind)
            for kind in (jnp.float32, jnp.bfloat16)
            for count in (slots, pad)
        ],
        compiler_params=pltpu.CompilerParams(vmem_limit_bytes=SMALL_LIMIT),
        name="attend",
    )(index, lengths, cache, *pieces)


def gather_kernel(token_size, index_ref, *rest):
    pieces, (out_ref, block_ref) = rest[:-2], rest[-2:]
    count = len(pieces)
    groups, query_rows, head_dim = pieces[0].shape
    heads = query_rows // token_size
    for shift in range(count):
        source = wrap(index_ref[1] + shift, count)
        for g in range(groups):
            wide = pieces[shift][g].astype(jnp.float32)
            for head in range(heads):
                lane = (g * heads + head) * head_dim
                block_ref[source, :, lane : lane + head_dim] = wide[
                    head * token_size : (head + 1) * token_size, :
                ]
    for lane in range(0, groups * heads * head_dim, head_dim):
        part = block_ref[:, :, lane : lane + head_dim].reshape(count * token_size, head_dim)
        out_ref[:, lane : lane + head_dim] = part.astype(jnp.bfloat16)


def gather(pieces, index, token_size):
    groups, query_rows, head_dim = pieces[0].shape
    width = groups * (query_rows // token_size) * head_dim
    return pl.pallas_call(
        functools.partial(gather_kernel, token_size),
        in_specs=[SMEM] + [VMEM] * len(pieces),
        out_specs=VMEM,
        out_shape=jax.ShapeDtypeStruct((len(pieces) * token_size, width), jnp.bfloat16),
        scratch_shapes=[pltpu.VMEM((len(pieces), token_size, width), jnp.float32)],
        compiler_params=pltpu.CompilerParams(vmem_limit_bytes=SMALL_LIMIT),
        name="gather",
    )(index, *pieces)


def hold_kernel(first, after_ref, through_ref, source_ref, held_ref, same_ref, arrived):
    rows = pl.ds(first, held_ref.shape[0])
    copy = pltpu.make_async_copy(source_ref.at[rows], held_ref, arrived)
    copy.start()
    copy.wait()


def hold(source, first, count, after, through):
    return pl.pallas_call(
        functools.partial(hold_kernel, first),
        in_specs=[pl.BlockSpec(memory_space=space) for space in (pl.ANY, pl.ANY, pltpu.HBM)],
        out_specs=[VMEM, pl.BlockSpec(memory_space=pl.ANY)],
        out_shape=[
            pltpu.VMEM((count, source.shape[1]), source.dtype),
            jax.ShapeDtypeStruct(through.shape, through.dtype),
        ],
        input_output_aliases={1: 1},
        scratch_shapes=[pltpu.SemaphoreType.DMA],
        compiler_params=pltpu.CompilerParams(vmem_limit_bytes=2**20),
        cost_estimate=pl.CostEstimate(
            flops=0, bytes_accessed=count * source.shape[1] * 2, transcendentals=0
        ),
        name="hold",
    )(after, through, in_hbm(source))


def outward_kernel(block_count, axis_size, begin, held_count, index_ref, weight_ref, *rest):
    held, rest = rest[:held_count], rest[held_count:]
    blocks, rest = rest[:block_count], rest[block_count:]
    outs, (left_ref, total_ref, buffer, arrived) = rest[:axis_size], rest[axis_size:]
    token_count, depth = left_ref.shape
    size = token_count // block_count
    steps, step, width = buffer.shape
    kept = sum(part.shape[0] for part in held)

    copies = [
        pltpu.make_async_copy(
            weight_ref.at[pl.ds(kept + k * step, step), pl.ds(begin, width)],
            buffer.at[k],
            arrived.at[k],
        )
        for k in range(steps)
    ]
    for copy in copies:
        copy.start()
    for shift in range(block_count):
        source = wrap(index_ref[0] + block_count - shift, block_count)
        left_ref[pl.ds(pl.multiple_of(source * size, size), size), :] = blocks[shift][...]
    first = 0
    for part in held:
        term = jnp.dot(
            left_ref[:, first : first + part.shape[0]],
            part[:, begin : begin + width],
            preferred_element_type=jnp.float32,
        )
        if first == 0:
            total_ref[...] = term
        else:
            total_ref[...] += term
        first += part.shape[0]

    for k in range(steps):
        copies[k].wait()
        total_ref[...] += jnp.dot(
            left_ref[:, first + k * step : first + (k + 1) * step],
            buffer[k],
            preferred_element_type=jnp.float32,
        )
    rows = token_count // axis_size
    for shift in range(axis_size):
        first = pl.multiple_of(wrap(index_ref[1] + axis_size - shift, axis_size) * rows, rows)
        outs[shift][...] = total_ref[pl.ds(first, rows), :].astype(outs[shift].dtype)


def outward(blocks, weight, held, begin, width, axis_size, index):
    size, depth = blocks[0].shape
    token_count = size * len(blocks)
    rows = token_count // axis_size
    streamed = depth - sum(part.shape[0] for part in held)
    steps = -(-streamed // OUTWARD_STEP)
    step = streamed // steps
    return pl.pallas_call(
        functools.partial(outward_kernel, len(blocks), axis_size, begin, len(held)),
        in_specs=[SMEM, pl.BlockSpec(memory_space=pltpu.HBM)] + [VMEM] * (len(held) + len(blocks)),
        out_specs=[VMEM] * axis_size,
        scratch_shapes=[
            pltpu.VMEM((token_count, depth), jnp.bfloat16),
            pltpu.VMEM((token_count, width), jnp.float32),
            pltpu.VMEM((steps, step, width), weight.dtype),
            pltpu.SemaphoreType.DMA((steps,)),
        ],
        out_shape=[
            jax.ShapeDtypeStruct((rows, width), jnp.bfloat16 if s else jnp.float32)
            for s in range(axis_size)
        ],
        compiler_params=pltpu.CompilerParams(vmem_limit_bytes=OUTWARD_LIMIT),
        cost_estimate=pl.CostEstimate(
            flops=2 * depth * width * token_count,
            bytes_accessed=2 * depth * width,
            transcendentals=0,
        ),
        name="outward",
    )(
        index,
        in_hbm(weight),
        *[pltpu.with_memory_space_constraint(part, pltpu.VMEM) for part in held],
        *blocks,
    )


def close_kernel(count, index_ref, tokens_ref, *rest):
    parts, out_ref = rest[:-1], rest[-1]
    rows, tokens, _ = out_ref.shape
    lanes = 128
    begin = 0
    for span in range(0, len(parts), count):
        width = parts[span].shape[1]
        for lane in range(0, width, lanes):
            total = parts[span][:, lane : lane + lanes]
            for part in parts[span + 1 : span + count]:
                total = total + part[:, lane : lane + lanes].astype(jnp.float32)
            at = begin + lane
            residual = tokens_ref[:, :, at : at + lanes].astype(jnp.float32)
            out_ref[:, :, at : at + lanes] = residual + total.reshape(rows, tokens, lanes)
        begin += width


def close(tokens, parts, head_devices, index):
    rows = tokens.shape[0] // head_devices
    shape = (rows,) + tokens.shape[1:]
    return pl.pallas_call(
        functools.partial(close_kernel, head_devices),
        grid_spec=pltpu.PrefetchScalarGridSpec(
            num_scalar_prefetch=1,
            grid=(1,),
            in_specs=[pl.BlockSpec(shape, lambda i, index: (index[1], 0, 0))]
            + [pl.BlockSpec(part.shape, lambda i, index: (0, 0)) for part in parts],
            out_specs=pl.BlockSpec(shape, lambda i, index: (0, 0, 0)),
        ),
        out_shape=jax.ShapeDtypeStruct(shape, jnp.float32),
        compiler_params=pltpu.CompilerParams(vmem_limit_bytes=SMALL_LIMIT),
        name="close",
    )(index, tokens, *parts)


def exchange(pieces, axis, sign=1):
    count = len(pieces)
    return [pieces[0]] + [
        lax.ppermute(pieces[s], axis, shift_pairs(count, sign * s)) for s in range(1, count)
    ]


def body(tokens, norm_gain, qkv_weight, out_weight, kv_cache, lengths, positions):
    rows_local = kv_cache.shape[0]
    width_devices = lax.axis_size("gx")
    head_devices = lax.axis_size("gy")
    index = jnp.stack([lax.axis_index("gx"), lax.axis_index("gy")])
    local_width = tokens.shape[2]
    head_dim = qkv_weight.shape[3]
    group_size = qkv_weight.shape[2] - 2
    token_size = rows_local * 2

    half = head_dim // 2
    frequency = rope_base ** (-2.0 * jnp.arange(half, dtype=jnp.float32) / head_dim)
    places = (positions[:, None] + jnp.arange(2, dtype=jnp.int32)[None, :]).astype(jnp.float32)
    angles = places.reshape(-1, 1) * frequency
    cosine = jnp.cos(angles)
    sine = jnp.sin(angles)
    cosine = jnp.concatenate([cosine, cosine], axis=1)
    sine = jnp.concatenate([-sine, sine], axis=1)
    cache = jnp.transpose(kv_cache, (0, 2, 3, 1, 4))

    parts = list(project(tokens, norm_gain, qkv_weight, width_devices, index))
    out_flat = out_weight.reshape(-1, local_width)
    cuts = [0]
    for share in HELD_SHARES:
        cuts.append(cuts[-1] + out_flat.shape[0] * share // 16)
    sizes = [end - begin for begin, end in zip(cuts, cuts[1:])]
    held = []

    def hold_beside(window, after, through):
        part, through = hold(out_flat, cuts[window], sizes[window], after, through)
        held.append(part)
        return through

    parts[0] = hold_beside(0, parts[1], parts[0])
    parts = exchange(parts, "gx")
    pieces = list(
        finish(parts, cosine, sine, cache, index, head_devices, token_size, head_dim)
    )
    pieces[0] = hold_beside(1, pieces[1], pieces[0])
    pieces = exchange(pieces, "gy")
    attended = list(attend(pieces, cache, lengths, index, group_size * token_size))
    attended[0] = hold_beside(2, attended[1], attended[0])
    attended = exchange(attended, "gy", -1)
    block = gather(attended, index, token_size)
    late = hold_beside(3, block, index + 0)
    blocks = exchange([block] * width_devices, "gx")
    cut = local_width * OUTWARD_SHARE // 16 // 128 * 128
    sums = []
    for begin, end in ((0, cut), (cut, local_width)):
        part = outward(blocks, out_flat, held, begin, end - begin, head_devices, late)
        sums += exchange(part, "gy", -1)
    return close(tokens, sums, head_devices, index)


def solution(mesh):
    return jax.shard_map(
        body,
        mesh=mesh,
        in_specs=(
            P("groups", None, "gx"),
            P("gx"),
            P("gx", "gy", None, None),
            P("gy", None, "gx"),
            P(("groups", "gx", "gy"), None, None, None, None),
            P(("groups", "gx", "gy")),
            P("groups"),
        ),
        out_specs=P(("groups", "gy"), None, "gx"),
        check_vma=False,
    )
```
